128 devices in a mesh: seq: 8 (over x, core), dp: 16 (over z, y).
Axes of the slice: x: 4, y: 4, z: 4, core: 2. Of those that a mesh axis runs over, the one named last changes fastest.
Arguments:
- queries: bfloat16 [16, 4096, 2048], P('dp', 'seq'), may hold values from -6 to 6
- keys: bfloat16 [16, 4096, 2048], P('dp', 'seq'), may hold values from -6 to 6
- values: bfloat16 [16, 4096, 2048], P('dp', 'seq'), may hold values from -6 to 6
- out_weight: bfloat16 [2048, 2048], replicated, may hold values from -0.125 to 0.125
- out_grad: bfloat16 [16, 4096, 2048], P('dp', 'seq'), may hold values from -6 to 6
Outputs:
- result: bfloat16 [16, 4096, 2048], P('dp', 'seq')
- grad_queries: bfloat16 [16, 4096, 2048], P('dp', 'seq')
- grad_keys: bfloat16 [16, 4096, 2048], P('dp', 'seq')
- grad_values: bfloat16 [16, 4096, 2048], P('dp', 'seq')
- grad_weight: float32 [2048, 2048], P(('seq', 'dp'))
The draws below stay inside these ranges and needn't reach their ends.
All inputs are finite; a program needn't handle non-finite values.
Results may differ from the reference program's by a relative error of at most 0.0052.
Values sent between devices are 32-bit elements; how exact they have to be, the bound alone decides.
A program may use at most 192 MiB of HBM per device.

```python
import jax
import jax.numpy as jnp
from jax import lax

HEADS = 16
DH = 128
DOUT = 2048
TOK_DEV = 512
HD = 2048
LENGTH = 4096
BATCH = 16


def level_of(stream_key, dims, cuts, least, top_value):
    factor_of = 1.0
    for dim, parts in cuts:
        draws = jax.random.uniform(jax.random.fold_in(jax.random.fold_in(stream_key, 6), dim), (parts,), jnp.float32, least / len(cuts), top_value / len(cuts))
        factor_of = factor_of * jnp.repeat(jnp.exp(draws), dims[dim] // parts).reshape((-1,) + (1,) * (len(dims) - 1 - dim))
    return factor_of


def gaussian(key, dims, deviation, bound, pieces=(), kind=jnp.bfloat16):
    gain = level_of(key, dims, pieces, -0.22, 0.18) if pieces else 1.0
    array = jax.random.normal(key, dims, jnp.float32) * deviation * gain
    return jnp.minimum(jnp.maximum(array, -bound), bound).astype(kind)


def setup_inputs(seed: int = 0) -> dict:
    seeds = jax.random.split(jax.random.key(seed), 6)
    queries = gaussian(seeds[0], (BATCH, LENGTH, HD), 1.0, 6.0, ((0, 16), (1, 8)))
    keys = gaussian(seeds[1], (BATCH, LENGTH, HD), 1.0, 6.0, ((0, 16), (1, 8)))
    values = gaussian(seeds[2], (BATCH, LENGTH, HD), 1.0, 6.0, ((0, 16), (1, 8)))
    out_weight = gaussian(seeds[3], (HD, DOUT), HD ** -0.5, 0.125)
    out_grad = gaussian(seeds[4], (BATCH, LENGTH, DOUT), 1.0, 6.0, ((0, 16), (1, 8)))
    return dict(queries=queries, keys=keys, values=values, out_weight=out_weight, out_grad=out_grad)


def reference(queries, keys, values, out_weight, out_grad):
    batch_count, length, feature_width = queries.shape
    num_blocks = length // TOK_DEV
    highest = lax.Precision.HIGHEST
    causal = jnp.arange(TOK_DEV)[:, None] >= jnp.arange(TOK_DEV)[None, :]

    def seq_pass(inputs):
        query_in, key_in, value_in, grad_in = inputs
        query_blocks = query_in.reshape(num_blocks, TOK_DEV, HEADS, DH)
        key_blocks = key_in.reshape(num_blocks, TOK_DEV, HEADS, DH)
        value_blocks = value_in.reshape(num_blocks, TOK_DEV, HEADS, DH)
        positions = jnp.arange(length, dtype=jnp.int32).reshape(num_blocks, TOK_DEV)
        row_scales = lax.rsqrt((DH * (positions + 1)).astype(jnp.float32))

        def forward_step(prefix_state, block_in):
            qblock, kblock, vblock, scale_row = block_in
            qfloat = qblock.astype(jnp.float32)
            kfloat = kblock.astype(jnp.float32)
            vfloat = vblock.astype(jnp.float32)
            scores = jnp.einsum('thd,shd->hts', qfloat, kfloat, precision=highest)
            weighted = (jnp.where(causal[None], scores, 0.0) * scale_row[None, :, None]).astype(jnp.bfloat16)
            inter = jnp.einsum('thd,hde->the', qfloat, prefix_state, precision=highest)
            intra = jnp.einsum('hts,she->the', weighted.astype(jnp.float32), vfloat, precision=highest)
            output_block = scale_row[:, None, None] * inter + intra
            new_state = prefix_state + jnp.einsum('shd,she->hde', kfloat, vfloat, precision=highest)
            return (new_state, (output_block.astype(jnp.bfloat16), prefix_state))
        empty_state = jnp.zeros((HEADS, DH, DH), jnp.float32)
        _, (out_blocks, prefix_states) = lax.scan(forward_step, empty_state, (query_blocks, key_blocks, value_blocks, row_scales))
        attended = out_blocks.reshape(length, feature_width)
        result = jnp.dot(attended, out_weight, preferred_element_type=jnp.float32).astype(jnp.bfloat16)
        grad_att = jnp.dot(grad_in, out_weight.T, preferred_element_type=jnp.float32).astype(jnp.bfloat16)
        grad_blocks = grad_att.reshape(num_blocks, TOK_DEV, HEADS, DH)

        def backward_step(suffix_state, block_in):
            qblock, kblock, vblock, gblock, scale_row, prefix_state = block_in
            qfloat = qblock.astype(jnp.float32)
            kfloat = kblock.astype(jnp.float32)
            vfloat = vblock.astype(jnp.float32)
            gfloat = gblock.astype(jnp.float32)
            scores = jnp.einsum('thd,shd->hts', qfloat, kfloat, precision=highest)
            weighted = (jnp.where(causal[None], scores, 0.0) * scale_row[None, :, None]).astype(jnp.bfloat16).astype(jnp.float32)
            raw_grad = jnp.where(causal[None], jnp.einsum('thd,shd->hts', gfloat, vfloat, precision=highest), 0.0)
            grad_scores = raw_grad.astype(jnp.bfloat16).astype(jnp.float32)
            scaled_grad = (raw_grad * scale_row[None, :, None]).astype(jnp.bfloat16).astype(jnp.float32)
            grad_q = scale_row[:, None, None] * (jnp.einsum('the,hde->thd', gfloat, prefix_state, precision=highest) + jnp.einsum('hts,shd->thd', grad_scores, kfloat, precision=highest))
            grad_k = jnp.einsum('she,hde->shd', vfloat, suffix_state, precision=highest) + jnp.einsum('hts,thd->shd', scaled_grad, qfloat, precision=highest)
            grad_v = jnp.einsum('shd,hde->she', kfloat, suffix_state, precision=highest) + jnp.einsum('hts,the->she', weighted, gfloat, precision=highest)
            new_state = suffix_state + jnp.einsum('thd,the->hde', qfloat * scale_row[:, None, None], gfloat, precision=highest)
            return (new_state, (grad_q.astype(jnp.bfloat16), grad_k.astype(jnp.bfloat16), grad_v.astype(jnp.bfloat16)))
        _, (grad_q, grad_k, grad_v) = lax.scan(backward_step, empty_state, (query_blocks, key_blocks, value_blocks, grad_blocks, row_scales, prefix_states), reverse=True)
        return (result, attended, grad_q.reshape(length, feature_width), grad_k.reshape(length, feature_width), grad_v.reshape(length, feature_width))
    results, attended_all, grad_queries, grad_keys, grad_values = lax.map(seq_pass, (queries, keys, values, out_grad))
    flat_att = attended_all.reshape(batch_count * length, feature_width)
    flat_grad = out_grad.reshape(batch_count * length, DOUT)
    grad_weight = jnp.dot(flat_att.T, flat_grad, preferred_element_type=jnp.float32) / jnp.sqrt(jnp.float32(batch_count * length))
    return (results, grad_queries, grad_keys, grad_values, grad_weight)
```

```python
import functools
import jax
import jax.numpy as jnp
from jax import lax
from jax.experimental import pallas as pl
from jax.experimental.pallas import tpu as pltpu
from jax.sharding import PartitionSpec as P

MESH = pl.DeviceIdType.MESH
TILES = 8
WIDE = 256
ORDERS = (("y", "z", "x"), ("z", "x", "y"), ("x", "y", "z"))
ALL = slice(None)


def place():
    s, d = lax.axis_index("seq"), lax.axis_index("dp")
    return {"x": s // 2, "c": s % 2, "z": d // 4, "y": d % 4}


def device(spot, **moves):
    spot = dict(spot)
    for axis, by in moves.items():
        spot[axis] = (spot[axis] + by) % (2 if axis == "c" else 4)
    return (spot["x"] * 2 + spot["c"], spot["z"] * 4 + spot["y"])


def greet(spot):
    barrier = pltpu.get_barrier_semaphore()
    partners = [device(spot, c=1)]
    for axis in "xyz":
        partners += [device(spot, **{axis: 1}), device(spot, **{axis: 3})]
    for partner in partners:
        pl.semaphore_signal(barrier, 1, device_id=partner, device_id_type=MESH)
    pl.semaphore_wait(barrier, len(partners))


class Scatter:
    def __init__(self, spot, lhs, rhs, out, refs, scale):
        (self.own, self.pair_out, self.pair_in, self.r1, self.r2, self.s1, self.s2,
         self.t1, self.t2, self.send, self.recv) = refs
        self.spot, self.lhs, self.rhs, self.out, self.scale = spot, lhs, rhs, out, scale

    def order(self, t):
        return ORDERS[t % 3]

    def view(self, t, sel, rows=ALL):
        return self.own.at[t, sel.get("x", ALL), sel.get("z", ALL), sel.get("y", ALL), rows]

    def copy(self, t, n, src, dst, **move):
        return pltpu.make_async_remote_copy(
            src_ref=src, dst_ref=dst, send_sem=self.send.at[t, n], recv_sem=self.recv.at[t, n],
            device_id=device(self.spot, **move), device_id_type=MESH)

    def pair(self, t):
        return self.copy(t, 0, self.pair_out.at[t % 3], self.pair_in.at[t], c=1)

    def parts(self, t, phase):
        axes = self.order(t)
        axis = axes[phase]
        me = self.spot[axis]
        fixed = {a: self.spot[a] for a in axes[:phase]}
        far = {**fixed, axis: (me + 2) % 4}
        after = {**fixed, axis: (me + 1) % 4}
        before = {**fixed, axis: (me + 3) % 4}
        rest = [a for a in "xzy" if a not in fixed and a != axis]
        if rest:
            lo, hi = {rest[0]: pl.ds(0, 2)}, {rest[0]: pl.ds(2, 2)}
            halves = lambda sel: (self.view(t, {**sel, **lo}), self.view(t, {**sel, **hi}))
        else:
            halves = lambda sel: (self.view(t, sel, pl.ds(0, 8)), self.view(t, sel, pl.ds(8, 8)))
        first = (self.r1, self.s1, self.t1)[phase].at[t]
        second = (self.r2, self.s2, self.t2)[phase].at[t]
        n = 1 + 4 * phase
        fa, fb = halves(far)

        def copies(i):
            src = (fa, fb, self.view(t, after), self.view(t, before))[i]
            dst = (first, first, second, second)[i].at[i % 2]
            return self.copy(t, n + i, src, dst, **{axis: 1 + 2 * (i % 2)})

        return copies, (halves(after)[0], halves(before)[1], self.view(t, {**fixed, axis: me})), (first, second)

    def partner_tile(self, t):
        if t >= 3:
            self.pair(t - 3).wait_send()
        c = self.spot["c"]
        cols = pl.ds(t * WIDE, WIDE)
        for xx in range(4):
            got = jnp.dot(self.lhs[xx, 1 - c], self.rhs[:, cols], preferred_element_type=jnp.float32)
            self.pair_out[t % 3, xx] = got.reshape(4, 4, 16, WIDE)
        self.pair(t).start()

    def own_tile(self, t):
        c = self.spot["c"]
        cols = pl.ds(t * WIDE, WIDE)
        self.pair(t).wait_recv()
        for xx in range(4):
            got = jnp.dot(self.lhs[xx, c], self.rhs[:, cols], preferred_element_type=jnp.float32)
            self.own[t, xx] = got.reshape(4, 4, 16, WIDE) + self.pair_in[t, xx]
        self.begin(t, 0)

    def begin(self, t, phase):
        copies, _, _ = self.parts(t, phase)
        copies(0).start()
        copies(1).start()

    def pass_on(self, t, phase):
        copies, (after, before, _), (first, _) = self.parts(t, phase)
        copies(0).wait_recv()
        after[...] = after[...] + first[0]
        copies(2).start()
        copies(1).wait_recv()
        before[...] = before[...] + first[1]
        copies(3).start()

    def finish(self, t, phase):
        copies, (_, _, mine), (_, second) = self.parts(t, phase)
        copies(2).wait_recv()
        copies(3).wait_recv()
        total = mine[...] + second[0] + second[1]
        if phase == 2:
            self.out[:, pl.ds(t * WIDE, WIDE)] = total * self.scale
        else:
            mine[...] = total
            self.begin(t, phase + 1)

    def drain(self):
        for t in range(TILES):
            if t >= TILES - 3:
                self.pair(t).wait_send()
            for phase in range(3):
                for i in range(4):
                    self.parts(t, phase)[0](i).wait_send()

    def events(self):
        out = []
        for t in range(TILES + 2):
            if t < TILES:
                out.append(functools.partial(self.partner_tile, t))
            if t >= 2:
                out.append(functools.partial(self.own_tile, t - 2))
        for phase in range(3):
            for t in range(TILES):
                out.append(functools.partial(self.pass_on, t, phase))
            for t in range(TILES):
                out.append(functools.partial(self.finish, t, phase))
        out.append(self.drain)
        return out

    @staticmethod
    def scratch():
        f32 = jnp.float32
        V = pltpu.VMEM
        return [
            V((TILES, 4, 4, 4, 16, WIDE), f32),
            V((3, 4, 4, 4, 16, WIDE), f32),
            V((TILES, 4, 4, 4, 16, WIDE), f32),
            V((TILES, 2, 2, 4, 16, WIDE), f32),
            V((TILES, 2, 4, 4, 16, WIDE), f32),
            V((TILES, 2, 2, 16, WIDE), f32),
            V((TILES, 2, 4, 16, WIDE), f32),
            V((TILES, 2, 8, WIDE), f32),
            V((TILES, 2, 16, WIDE), f32),
            pltpu.SemaphoreType.DMA((TILES, 13)),
            pltpu.SemaphoreType.DMA((TILES, 13)),
        ]


def weight_kernel(scale, att, grad, out, lhs, *refs):
    spot = place()
    greet(spot)
    for head in range(16):
        lhs[head // 4, head % 4 // 2, pl.ds(head % 2 * 128, 128)] = att[:, pl.ds(head * 128, 128)].T
    for event in Scatter(spot, lhs, grad, out, refs, scale).events():
        event()


def weight_grad(att, grad, scale):
    return pl.pallas_call(
        functools.partial(weight_kernel, scale),
        out_shape=jax.ShapeDtypeStruct((16, 2048), jnp.float32),
        in_specs=[pl.BlockSpec(memory_space=pltpu.VMEM)] * 2,
        out_specs=pl.BlockSpec(memory_space=pltpu.VMEM),
        scratch_shapes=[pltpu.VMEM((4, 2, 256, 512), jnp.bfloat16)] + Scatter.scratch(),
        compiler_params=pltpu.CompilerParams(
            collective_id=0, has_side_effects=True, vmem_limit_bytes=60 * 2**20),
    )(att, grad)


HEADS = 16
DH = 128
DOUT = 2048


def prefix(value, axis, join, neutral, backward):
    count, mine = (lax.axis_size(axis), lax.axis_index(axis))
    pieces = lax.all_gather(value, axis)
    if backward:
        pieces = pieces[::-1]
        mine = count - 1 - mine
    subtotal = jnp.full_like(value, 0) + jnp.asarray(neutral, value.dtype)

    def step(position, subtotal):
        longer = join(subtotal, pieces[position])
        return jnp.where(position < mine, longer, subtotal)

    return lax.fori_loop(0, count - 1, step, subtotal)


def add_states(earlier, later):
    return earlier + later


def local(queries, keys, values, out_weight, out_grad):
    tok_rows = queries.shape[1]
    feature_width = queries.shape[2]
    highest = lax.Precision.HIGHEST
    query_heads = queries.reshape(tok_rows, HEADS, DH)
    key_heads = keys.reshape(tok_rows, HEADS, DH)
    value_heads = values.reshape(tok_rows, HEADS, DH)
    grad_rows = out_grad.reshape(tok_rows, DOUT)
    my_index = lax.axis_index("seq")
    positions = my_index * tok_rows + jnp.arange(tok_rows, dtype=jnp.int32)
    row_scale = lax.rsqrt((DH * (positions + 1)).astype(jnp.float32))
    causal = jnp.arange(tok_rows)[:, None] >= jnp.arange(tok_rows)[None, :]
    empty_state = jnp.zeros((HEADS, DH, DH), jnp.float32)
    local_state = jnp.einsum(
        "shd,she->hde", key_heads, value_heads, preferred_element_type=jnp.float32
    )
    prefix_state = prefix(local_state, "seq", add_states, empty_state, False)
    query_float = query_heads.astype(jnp.float32)
    scores = jnp.einsum("thd,shd->hts", query_heads, key_heads, preferred_element_type=jnp.float32)
    weighted = (jnp.where(causal[None], scores, 0.0) * row_scale[None, :, None]).astype(
        jnp.bfloat16
    )
    inter = jnp.einsum("thd,hde->the", query_float, prefix_state, precision=highest)
    intra = jnp.einsum("hts,she->the", weighted, value_heads, preferred_element_type=jnp.float32)
    attended = (
        (row_scale[:, None, None] * inter + intra)
        .astype(jnp.bfloat16)
        .reshape(tok_rows, feature_width)
    )
    result = jnp.dot(attended, out_weight, preferred_element_type=jnp.float32).astype(jnp.bfloat16)
    grad_att = jnp.dot(grad_rows, out_weight.T, preferred_element_type=jnp.float32).astype(
        jnp.bfloat16
    )
    grad_heads = grad_att.reshape(tok_rows, HEADS, DH)
    grad_float = grad_heads.astype(jnp.float32)
    local_grad = jnp.einsum(
        "thd,the->hde", query_float * row_scale[:, None, None], grad_float, precision=highest
    )
    suffix_state = prefix(local_grad, "seq", add_states, empty_state, True)
    raw_grad = jnp.where(
        causal[None],
        jnp.einsum("thd,shd->hts", grad_heads, value_heads, preferred_element_type=jnp.float32),
        0.0,
    )
    grad_scores = raw_grad.astype(jnp.bfloat16)
    scaled_grad = (raw_grad * row_scale[None, :, None]).astype(jnp.bfloat16)
    grad_q = row_scale[:, None, None] * (
        jnp.einsum("the,hde->thd", grad_float, prefix_state, precision=highest)
        + jnp.einsum("hts,shd->thd", grad_scores, key_heads, preferred_element_type=jnp.float32)
    )
    grad_k = jnp.einsum(
        "she,hde->shd", value_heads.astype(jnp.float32), suffix_state, precision=highest
    ) + jnp.einsum("hts,thd->shd", scaled_grad, query_heads, preferred_element_type=jnp.float32)
    grad_v = jnp.einsum(
        "shd,hde->she", key_heads.astype(jnp.float32), suffix_state, precision=highest
    ) + jnp.einsum("hts,the->she", weighted, grad_heads, preferred_element_type=jnp.float32)
    norm_factor = (lax.axis_size("dp") * lax.axis_size("seq") * tok_rows) ** -0.5
    grad_weight = weight_grad(attended, grad_rows, norm_factor)
    return (
        result.reshape(1, tok_rows, DOUT),
        grad_q.astype(jnp.bfloat16).reshape(1, tok_rows, feature_width),
        grad_k.astype(jnp.bfloat16).reshape(1, tok_rows, feature_width),
        grad_v.astype(jnp.bfloat16).reshape(1, tok_rows, feature_width),
        grad_weight,
    )


def solution(mesh):
    in_specs = (
        P("dp", "seq", None),
        P("dp", "seq", None),
        P("dp", "seq", None),
        P(),
        P("dp", "seq", None),
    )
    out_specs = (
        P("dp", "seq", None),
        P("dp", "seq", None),
        P("dp", "seq", None),
        P("dp", "seq", None),
        P(("seq", "dp"), None),
    )
    return jax.shard_map(local, mesh=mesh, in_specs=in_specs, out_specs=out_specs, check_vma=False)
```

```python
import functools

import jax
import jax.numpy as jnp
from jax import lax
from jax.experimental import pallas as pl
from jax.experimental.pallas import tpu as pltpu
from jax.sharding import PartitionSpec as P

MESH = pl.DeviceIdType.MESH
HEADS = 16
HALF = 8
DH = 128
TOK = 512
MID = 256
HD = 2048
TILES = 8
WIDE = 256
LAG = 2
ORDERS = (("y", "z", "x"), ("z", "x", "y"), ("x", "y", "z"))
ALL = slice(None)
A, B = pl.ds(0, MID), pl.ds(MID, MID)
f32, bf16 = jnp.float32, jnp.bfloat16


def place():
    s, d = lax.axis_index("seq"), lax.axis_index("dp")
    return {"x": s // 2, "c": s % 2, "z": d // 4, "y": d % 4}


def device(spot, **moves):
    spot = dict(spot)
    for axis, by in moves.items():
        spot[axis] = (spot[axis] + by) % (2 if axis == "c" else 4)
    return (spot["x"] * 2 + spot["c"], spot["z"] * 4 + spot["y"])


def greet(spot):
    barrier = pltpu.get_barrier_semaphore()
    partners = [device(spot, c=1)]
    for axis in "xyz":
        partners += [device(spot, **{axis: 1}), device(spot, **{axis: 3})]
    for partner in partners:
        pl.semaphore_signal(barrier, 1, device_id=partner, device_id_type=MESH)
    pl.semaphore_wait(barrier, len(partners))


def dot(a, b):
    return jnp.dot(a, b, preferred_element_type=f32)


def dot_nt(a, b):
    return lax.dot_general(a, b, (((1,), (1,)), ((), ())), preferred_element_type=f32)


def lanes(h, size=DH):
    return pl.ds(h * size if isinstance(h, int) else pl.multiple_of(h * size, size), size)


def two(value):
    high = value.astype(bf16)
    return high, (value - high.astype(f32)).astype(bf16)


class Flow:
    def __init__(self, spot, refs, backward):
        self.local, self.pair_in, self.chain_in, self.chain_out, self.share_out, self.state, self.send, self.recv = refs
        self.spot, self.c = spot, spot["c"]
        self.rank = 3 - spot["x"] if backward else spot["x"]
        self.move = 3 if backward else 1
        self.first = (self.c == (1 if backward else 0)).astype(f32)

    @staticmethod
    def scratch():
        full, half = pltpu.VMEM((HEADS, DH, DH), f32), pltpu.VMEM((HALF, DH, DH), f32)
        sems = pltpu.SemaphoreType.DMA((3, HALF))
        return [full, half, half, half, half, full, sems, sems]

    def copy(self, kind, i, src, dst, **move):
        return pltpu.make_async_remote_copy(
            src_ref=src, dst_ref=dst, send_sem=self.send.at[kind, i], recv_sem=self.recv.at[kind, i],
            device_id=device(self.spot, **move), device_id_type=MESH)

    def pair(self, i):
        return self.copy(0, i, self.local.at[HALF * (1 - self.c) + i], self.pair_in.at[i], c=1)

    def chain(self, i):
        return self.copy(1, i, self.chain_out.at[i], self.chain_in.at[i], x=self.move)

    def share(self, i):
        return self.copy(2, i, self.share_out.at[i], self.state.at[HALF * self.c + i], c=1)

    def clear(self):
        @pl.when(self.rank == 0)
        def _():
            self.chain_in[...] = jnp.zeros_like(self.chain_in)

    def step(self, i):
        mine = HALF * self.c + i
        self.pair(i).wait_recv()

        @pl.when(self.rank > 0)
        def _():
            self.chain(i).wait_recv()

        @pl.when(self.rank < 3)
        def _():
            self.chain_out[i] = self.chain_in[i] + (self.local[mine] + self.pair_in[i])
            self.chain(i).start()

        self.share_out[i] = self.chain_in[i] + self.first * self.local[mine]
        self.share(i).start()
        self.state[mine] = self.chain_in[i] + (1.0 - self.first) * self.pair_in[i]

    def drain(self):
        for i in range(HALF):
            self.pair(i).wait_send()
            self.share(i).wait_send()

        @pl.when(self.rank < 3)
        def _():
            for i in range(HALF):
                self.chain(i).wait_send()


class Scatter:
    def __init__(self, spot, lhs, rhs, out, refs, scale):
        (self.own, self.pair_out, self.r1, self.r2, self.s1, self.s2,
         self.t1, self.t2, self.send, self.recv) = refs
        self.spot, self.lhs, self.rhs, self.out, self.scale = spot, lhs, rhs, out, scale

    def order(self, t):
        return ORDERS[t % 3]

    def view(self, t, sel, rows=ALL):
        return self.own.at[t, sel.get("x", ALL), sel.get("z", ALL), sel.get("y", ALL), rows]

    def copy(self, t, n, src, dst, **move):
        return pltpu.make_async_remote_copy(
            src_ref=src, dst_ref=dst, send_sem=self.send.at[t, n], recv_sem=self.recv.at[t, n],
            device_id=device(self.spot, **move), device_id_type=MESH)

    def pair(self, t):
        return self.copy(t, 0, self.pair_out.at[t % 3], self.own.at[t], c=1)

    def parts(self, t, phase):
        axes = self.order(t)
        axis = axes[phase]
        me = self.spot[axis]
        fixed = {a: self.spot[a] for a in axes[:phase]}
        far = {**fixed, axis: (me + 2) % 4}
        after = {**fixed, axis: (me + 1) % 4}
        before = {**fixed, axis: (me + 3) % 4}
        rest = [a for a in "xzy" if a not in fixed and a != axis]
        if rest:
            lo, hi = {rest[0]: pl.ds(0, 2)}, {rest[0]: pl.ds(2, 2)}
            halves = lambda sel: (self.view(t, {**sel, **lo}), self.view(t, {**sel, **hi}))
        else:
            halves = lambda sel: (self.view(t, sel, pl.ds(0, 8)), self.view(t, sel, pl.ds(8, 8)))
        first = (self.r1, self.s1, self.t1)[phase].at[t]
        second = (self.r2, self.s2, self.t2)[phase].at[t]
        n = 1 + 4 * phase
        fa, fb = halves(far)

        def copies(i):
            src = (fa, fb, self.view(t, after), self.view(t, before))[i]
            dst = (first, first, second, second)[i].at[i % 2]
            return self.copy(t, n + i, src, dst, **{axis: 1 + 2 * (i % 2)})

        return copies, (halves(after)[0], halves(before)[1], self.view(t, {**fixed, axis: me})), (first, second)

    def partner_tile(self, t):
        if t >= 3:
            self.pair(t - 3).wait_send()
        c = self.spot["c"]
        for xx in range(4):
            got = dot(self.lhs[xx, 1 - c], self.rhs[:, lanes(t, WIDE)])
            self.pair_out[t % 3, xx] = got.reshape(4, 4, 16, WIDE)
        self.pair(t).start()

    def own_tile(self, t):
        c = self.spot["c"]
        self.pair(t).wait_recv()
        for xx in range(4):
            got = dot(self.lhs[xx, c], self.rhs[:, lanes(t, WIDE)])
            self.own[t, xx] = self.own[t, xx] + got.reshape(4, 4, 16, WIDE)
        self.begin(t, 0)

    def begin(self, t, phase):
        copies, _, _ = self.parts(t, phase)
        copies(0).start()
        copies(1).start()

    def pass_on(self, t, phase):
        copies, (after, before, _), (first, _) = self.parts(t, phase)
        copies(0).wait_recv()
        after[...] = after[...] + first[0]
        copies(2).start()
        copies(1).wait_recv()
        before[...] = before[...] + first[1]
        copies(3).start()

    def finish(self, t, phase):
        copies, (_, _, mine), (_, second) = self.parts(t, phase)
        copies(2).wait_recv()
        copies(3).wait_recv()
        total = mine[...] + second[0] + second[1]
        if phase == 2:
            self.out[:, lanes(t, WIDE)] = total * self.scale
        else:
            mine[...] = total
            self.begin(t, phase + 1)

    def drain(self):
        for t in range(TILES):
            if t >= TILES - 3:
                self.pair(t).wait_send()
            for phase in range(3):
                for i in range(4):
                    self.parts(t, phase)[0](i).wait_send()

    def products(self):
        out = []
        for t in range(TILES + 2):
            if t < TILES:
                out.append(functools.partial(self.partner_tile, t))
            if t >= 2:
                out.append(functools.partial(self.own_tile, t - 2))
        return out

    def hops(self, phase):
        out = [functools.partial(self.pass_on, t, phase) for t in range(TILES)]
        return out + [functools.partial(self.finish, t, phase) for t in range(TILES)]

    @staticmethod
    def scratch():
        V = pltpu.VMEM
        return [
            V((TILES, 4, 4, 4, 16, WIDE), f32),
            V((3, 4, 4, 4, 16, WIDE), f32),
            V((TILES, 2, 2, 4, 16, WIDE), f32),
            V((TILES, 2, 4, 4, 16, WIDE), f32),
            V((TILES, 2, 2, 16, WIDE), f32),
            V((TILES, 2, 4, 16, WIDE), f32),
            V((TILES, 2, 8, WIDE), f32),
            V((TILES, 2, 16, WIDE), f32),
            pltpu.SemaphoreType.DMA((TILES, 13)),
            pltpu.SemaphoreType.DMA((TILES, 13)),
        ]


FLOW = len(Flow.scratch())
SCATTER = len(Scatter.scratch())


def layer(scale, q_in, k_in, v_in, w_in, og_in, res_out, gq_out, gk_out, gv_out, gw_out, *refs):
    (q, k, v, og, g, att, att_t, intra, wrow, wcol, col, tri, tri_t, ctri, ctri_t, crow,
     in_sem, row_sem, col_sem, out_sem) = refs[:20]
    pre_refs, suf_refs, sc_refs = refs[20:20 + FLOW], refs[20 + FLOW:20 + 2 * FLOW], refs[20 + 2 * FLOW:]
    spot = place()
    c = spot["c"]
    pre, suf = Flow(spot, pre_refs, False), Flow(spot, suf_refs, True)
    scatter = Scatter(spot, att_t, og, gw_out, sc_refs, scale)

    def load(n, src, dst, part):
        cols = pl.ds(pl.multiple_of(part * 1024, 1024), 1024)
        return pltpu.make_async_copy(src.at[:, cols], dst.at[:, cols], in_sem.at[n])

    theirs, ours = 1 - c, c
    loads = {}
    for n, (name, src, dst, part) in enumerate((
            ("k0", k_in, k, theirs), ("v0", v_in, v, theirs), ("k1", k_in, k, ours), ("v1", v_in, v, ours),
            ("q0", q_in, q, theirs), ("q1", q_in, q, ours), ("og0", og_in, og, theirs), ("og1", og_in, og, ours))):
        loads[name] = load(n, src, dst, part)

    def tile_of(p):
        return (p + 4 * theirs) % 8

    def row_tile(p):
        rows = pl.ds(pl.multiple_of(tile_of(p) * WIDE, WIDE), WIDE)
        return pltpu.make_async_copy(w_in.at[rows], wrow.at[p % 3], row_sem.at[p])

    def col_tile(n):
        return pltpu.make_async_copy(w_in.at[:, lanes(n, WIDE)], wcol.at[n % 2], col_sem.at[n])

    for name in ("k0", "v0", "k1", "v1", "q0", "q1"):
        loads[name].start()
    row_tile(0).start()
    loads["og0"].start()
    loads["og1"].start()
    row_tile(1).start()
    row_tile(2).start()

    base = lax.axis_index("seq") * TOK + 1

    def scale_of(shape, dim):
        index = lax.broadcasted_iota(jnp.int32, shape, dim)
        return lax.rsqrt((DH * (index + base)).astype(f32))

    col[...] = scale_of((TOK, DH), 0)
    crow[...] = scale_of((8, TOK), 1)
    below = (lax.broadcasted_iota(jnp.int32, (MID, MID), 0) >= lax.broadcasted_iota(jnp.int32, (MID, MID), 1)).astype(f32)
    above = (lax.broadcasted_iota(jnp.int32, (MID, MID), 0) <= lax.broadcasted_iota(jnp.int32, (MID, MID), 1)).astype(f32)
    tri[...] = below
    for b, rows in enumerate((A, B)):
        ctri[b] = jnp.concatenate([col[rows]] * 2, axis=1) * below
        ctri_t[b] = crow[0:1, rows] * above
    pre.clear()
    suf.clear()
    greet(spot)

    def local_state(h):
        pre.local[h] = dot(k[:, lanes(h)].T, v[:, lanes(h)])

    def local_grad(h):
        high, low = two(col[...] * q[:, lanes(h)].astype(f32))
        both = dot(g[:, lanes(h)].T, jnp.concatenate([high, low], axis=1))
        suf.local[h] = both[:, :DH] + both[:, DH:]

    def attend_intra(h):
        hs = lanes(h)
        c_b = jnp.concatenate([col[B]] * 2, axis=1)
        w_a = (dot_nt(q[A, hs], k[A, hs]) * ctri[0]).astype(bf16)
        w_ba = (dot_nt(q[B, hs], k[A, hs]) * c_b).astype(bf16)
        w_bb = (dot_nt(q[B, hs], k[B, hs]) * ctri[1]).astype(bf16)
        intra[h, A] = dot(w_a, v[A, hs])
        intra[h, B] = dot(jnp.concatenate([w_ba, w_bb], axis=1), v[:, hs])

    def attend(h):
        hs = lanes(h)
        high, low = two(pre.state[h])
        x = q[:, hs]
        inter = dot(jnp.concatenate([x, x], axis=1), jnp.concatenate([high, low], axis=0))
        got = (col[...] * inter + intra[h]).astype(bf16)
        att[:, hs] = got
        att_t[h // 4, h % 4 // 2, lanes(h % 2)] = got.T

    def grad_att(p):
        row_tile(p).wait()
        n = tile_of(p)
        g[:, lanes(n, WIDE)] = dot_nt(og[...], wrow[p % 3]).astype(bf16)
        if p + 3 < TILES:
            row_tile(p + 3).start()
        local_grad(2 * n)
        local_grad(2 * n + 1)
        if p < 4:
            suf.pair(2 * p).start()
            suf.pair(2 * p + 1).start()

    def back(h):
        hs = lanes(h)
        ga, gb, va, vb, ka, kb, qa, qb = (r[s, hs] for r in (g, v, k, q) for s in (A, B))
        gg, vv, kk, qq = g[:, hs], v[:, hs], k[:, hs], q[:, hs]
        c_b = crow[0:1, B]
        r_a = (dot_nt(ga, va) * tri[...]).astype(bf16)
        r_ba = dot_nt(gb, va).astype(bf16)
        r_bb = (dot_nt(gb, vb) * tri[...]).astype(bf16)
        high, low = two(pre.state[h])
        inter = dot_nt(jnp.concatenate([gg, gg], axis=1), jnp.concatenate([high, low], axis=1))
        gq_a = (col[A] * (inter[:MID] + dot(r_a, ka))).astype(bf16)
        gq_b = (col[B] * (inter[MID:] + dot(jnp.concatenate([r_ba, r_bb], axis=1), kk))).astype(bf16)
        high, low = two(suf.state[h])
        s_aa = (dot_nt(va, ga) * ctri_t[0]).astype(bf16)
        s_ab = (dot_nt(va, gb) * c_b).astype(bf16)
        s_bb = (dot_nt(vb, gb) * ctri_t[1]).astype(bf16)
        inter = dot(jnp.concatenate([vv, vv], axis=1), jnp.concatenate([high, low], axis=0))
        gk_a = (inter[:MID] + dot(jnp.concatenate([s_aa, s_ab], axis=1), qq)).astype(bf16)
        gk_b = (inter[MID:] + dot(s_bb, qb)).astype(bf16)
        w_aa = (dot_nt(ka, qa) * ctri_t[0]).astype(bf16)
        w_ab = (dot_nt(ka, qb) * c_b).astype(bf16)
        w_bb = (dot_nt(kb, qb) * ctri_t[1]).astype(bf16)
        inter = dot_nt(jnp.concatenate([kk, kk], axis=1), jnp.concatenate([high, low], axis=1))
        gv_a = (inter[:MID] + dot(jnp.concatenate([w_aa, w_ab], axis=1), gg)).astype(bf16)
        gv_b = (inter[MID:] + dot(w_bb, gb)).astype(bf16)
        q[A, hs], q[B, hs] = gq_a, gq_b
        k[A, hs], k[B, hs] = gk_a, gk_b
        v[A, hs], v[B, hs] = gv_a, gv_b
        for n in range(3):
            head_out(n, h).start()

    def head_out(n, h):
        src, dst = ((q, gq_out), (k, gk_out), (v, gv_out))[n]
        return pltpu.make_async_copy(src.at[:, lanes(h)], dst.at[:, lanes(h)], out_sem.at[n, h])

    def result_out(n):
        return pltpu.make_async_copy(og.at[:, lanes(n, WIDE)], res_out.at[:, lanes(n, WIDE)], out_sem.at[3, n])

    def result(n):
        col_tile(n).wait()
        og[:, lanes(n, WIDE)] = dot(att[...], wcol[n % 2]).astype(bf16)
        result_out(n).start()
        if n + 2 < TILES:
            col_tile(n + 2).start()

    loads["k0"].wait()
    loads["v0"].wait()
    for i in range(HALF):
        local_state(HALF * theirs + i)
        pre.pair(i).start()
    loads["k1"].wait()
    loads["v1"].wait()
    for i in range(HALF):
        local_state(HALF * ours + i)
    for name in ("q0", "q1"):
        loads[name].wait()

    def when_in(i, body):
        pl.when(jnp.logical_and(i >= 0, i < HALF))(lambda: body(i))

    def after_step(i):
        attend(HALF * c + i)

    def after_share(i):
        pre.share(i).wait_recv()
        attend(HALF * (1 - c) + i)

    def suffix_step(p):
        when_in(p - HALF - LAG * suf.rank, suf.step)

    col_tile(0).start()
    col_tile(1).start()
    last = HALF + 3 * LAG + 1
    for p in range(last):
        i = p - LAG * pre.rank
        when_in(i, pre.step)
        if p < TILES:
            attend_intra(p)
            attend_intra(HALF + p)
            if p == 0:
                loads["og0"].wait()
                loads["og1"].wait()
            grad_att(p)
        when_in(i, after_step)
        when_in(i - 1, after_share)
        suffix_step(p)

    for event in scatter.products():
        event()
    for p in range(last, last + HALF):
        suffix_step(p)
    for i in range(HALF):
        suf.share(i).wait_recv()
    work = []
    for n in range(TILES):
        work += [functools.partial(result, n), functools.partial(back, 2 * n), functools.partial(back, 2 * n + 1)]
    hops = scatter.hops(0) + scatter.hops(1) + scatter.hops(2)
    at = 0
    for n, hop in enumerate(hops):
        upto = min(len(work), -(-len(work) * (n + 1) // 24))
        for unit in work[at:upto]:
            unit()
        at = upto
        hop()
    scatter.drain()
    pre.drain()
    suf.drain()
    for n in range(3):
        for h in range(HEADS):
            head_out(n, h).wait()
    for n in range(TILES):
        result_out(n).wait()


def local(queries, keys, values, out_weight, out_grad):
    tokens = lax.axis_size("dp") * lax.axis_size("seq") * TOK
    wide = lambda: pltpu.VMEM((TOK, HD), bf16)
    hbm = pl.BlockSpec(memory_space=pl.ANY)
    rows = jax.ShapeDtypeStruct((TOK, HD), bf16)
    sem = pltpu.SemaphoreType.DMA
    outs = pl.pallas_call(
        functools.partial(layer, float(tokens) ** -0.5),
        out_shape=[rows] * 4 + [jax.ShapeDtypeStruct((16, HD), f32)],
        in_specs=[hbm] * 5,
        out_specs=[hbm] * 4 + [pl.BlockSpec(memory_space=pltpu.VMEM)],
        scratch_shapes=[
            wide(), wide(), wide(), wide(), wide(), wide(),
            pltpu.VMEM((4, 2, 256, TOK), bf16),
            pltpu.VMEM((HEADS, TOK, DH), f32),
            pltpu.VMEM((3, WIDE, HD), bf16),
            pltpu.VMEM((2, HD, WIDE), bf16),
            pltpu.VMEM((TOK, DH), f32),
            pltpu.VMEM((MID, MID), f32),
            pltpu.VMEM((MID, MID), f32),
            pltpu.VMEM((2, MID, MID), f32),
            pltpu.VMEM((2, MID, MID), f32),
            pltpu.VMEM((8, TOK), f32),
            sem((8,)), sem((TILES,)), sem((TILES,)), sem((4, HEADS)),
        ] + Flow.scratch() + Flow.scratch() + Scatter.scratch(),
        compiler_params=pltpu.CompilerParams(collective_id=0, has_side_effects=True, vmem_limit_bytes=60 * 2**20),
        cost_estimate=pl.CostEstimate(flops=23 * 10**9, bytes_accessed=25 * 10**6, transcendentals=0),
    )(*(x.reshape(TOK, HD) for x in (queries, keys, values)), out_weight, out_grad.reshape(TOK, HD))
    return tuple(x.reshape(1, TOK, HD) for x in outs[:4]) + (outs[4],)


def solution(mesh):
    in_specs = (
        P("dp", "seq", None),
        P("dp", "seq", None),
        P("dp", "seq", None),
        P(),
        P("dp", "seq", None),
    )
    out_specs = (
        P("dp", "seq", None),
        P("dp", "seq", None),
        P("dp", "seq", None),
        P("dp", "seq", None),
        P(("seq", "dp"), None),
    )
    return jax.shard_map(local, mesh=mesh, in_specs=in_specs, out_specs=out_specs, check_vma=False)
```

```python
import functools

import jax
import jax.numpy as jnp
from jax import lax
from jax.experimental import pallas as pl
from jax.experimental.pallas import tpu as pltpu
from jax.sharding import PartitionSpec as P

MESH = pl.DeviceIdType.MESH
HEADS = 16
HALF = 8
DH = 128
TOK = 512
MID = 256
HD = 2048
TILES = 8
WIDE = 256
LAG = 2
Y_FIRST, Z_FIRST, X_FIRST = ("y", "z", "x"), ("z", "x", "y"), ("x", "y", "z")
ORDERS = (Y_FIRST, Z_FIRST, X_FIRST)
ALL = slice(None)
A, B = pl.ds(0, MID), pl.ds(MID, MID)
f32, bf16 = jnp.float32, jnp.bfloat16


def place():
    s, d = lax.axis_index("seq"), lax.axis_index("dp")
    return {"x": s // 2, "c": s % 2, "z": d // 4, "y": d % 4}


def device(spot, **moves):
    spot = dict(spot)
    for axis, by in moves.items():
        spot[axis] = (spot[axis] + by) % (2 if axis == "c" else 4)
    return (spot["x"] * 2 + spot["c"], spot["z"] * 4 + spot["y"])


def greet(spot):
    barrier = pltpu.get_barrier_semaphore()
    partners = [device(spot, c=1)]
    for axis in "xyz":
        partners += [device(spot, **{axis: by}) for by in (1, 2, 3)]
    for partner in partners:
        pl.semaphore_signal(barrier, 1, device_id=partner, device_id_type=MESH)
    return lambda: pl.semaphore_wait(barrier, len(partners))


def dot(a, b):
    return jnp.dot(a, b, preferred_element_type=f32)


def dot_nt(a, b):
    return lax.dot_general(a, b, (((1,), (1,)), ((), ())), preferred_element_type=f32)


def lanes(h, size=DH):
    return pl.ds(h * size if isinstance(h, int) else pl.multiple_of(h * size, size), size)


def two(value):
    high = value.astype(bf16)
    return high, (value - high.astype(f32)).astype(bf16)


class Flow:
    def __init__(self, spot, refs, backward):
        self.local, self.pair_in, self.chain_in, self.chain_out, self.share_out, self.state, self.send, self.recv = refs
        self.spot, self.c = spot, spot["c"]
        self.rank = 3 - spot["x"] if backward else spot["x"]
        self.move = 3 if backward else 1
        self.first = (self.c == (1 if backward else 0)).astype(f32)

    @staticmethod
    def scratch():
        full, half = pltpu.VMEM((HEADS, DH, DH), f32), pltpu.VMEM((HALF, DH, DH), f32)
        sems = pltpu.SemaphoreType.DMA((3, HALF))
        return [full, half, half, half, half, full, sems, sems]

    def copy(self, kind, i, src, dst, **move):
        return pltpu.make_async_remote_copy(
            src_ref=src, dst_ref=dst, send_sem=self.send.at[kind, i], recv_sem=self.recv.at[kind, i],
            device_id=device(self.spot, **move), device_id_type=MESH)

    def pair(self, i):
        return self.copy(0, i, self.local.at[HALF * (1 - self.c) + i], self.pair_in.at[i], c=1)

    def chain(self, i):
        return self.copy(1, i, self.chain_out.at[i], self.chain_in.at[i], x=self.move)

    def share(self, i):
        return self.copy(2, i, self.share_out.at[i], self.state.at[HALF * self.c + i], c=1)

    def clear(self):
        @pl.when(self.rank == 0)
        def _():
            self.chain_in[...] = jnp.zeros_like(self.chain_in)

    def step(self, i):
        mine = HALF * self.c + i
        self.pair(i).wait_recv()

        @pl.when(self.rank > 0)
        def _():
            self.chain(i).wait_recv()

        @pl.when(self.rank < 3)
        def _():
            self.chain_out[i] = self.chain_in[i] + (self.local[mine] + self.pair_in[i])
            self.chain(i).start()

        self.share_out[i] = self.chain_in[i] + self.first * self.local[mine]
        self.share(i).start()
        self.state[mine] = self.chain_in[i] + (1.0 - self.first) * self.pair_in[i]

    def due(self, p, start=0):
        late = jnp.maximum(p - 3 * self.rank, 0)
        return jnp.where(self.rank == 0, jnp.where(p <= start, 0, HALF), jnp.minimum((2 * late + 2) // 3, HALF))

    def steps(self, p, start=0):
        lax.fori_loop(self.due(p, start), self.due(p + 1, start), lambda i, _: self.step(i), None)

    def drain(self):
        @pl.loop(0, HALF)
        def _(i):
            self.pair(i).wait_send()
            self.share(i).wait_send()

            @pl.when(self.rank < 3)
            def _():
                self.chain(i).wait_send()


class Scatter:
    def __init__(self, spot, lhs, rhs, out, refs, scale):
        (self.own, self.pair_out, self.r1, self.r2, self.s2,
         self.t2, self.send, self.recv) = refs
        self.spot, self.lhs, self.rhs, self.out, self.scale = spot, lhs, rhs, out, scale

    def each(self, t, body):
        kind = jnp.where(t < 6, t % 2, 2)
        for n, axes in enumerate(ORDERS):
            pl.when(kind == n)(functools.partial(body, axes))

    def view(self, t, sel, rows=ALL):
        return self.own.at[t, sel.get("x", ALL), sel.get("z", ALL), sel.get("y", ALL), rows]

    def copy(self, t, n, src, dst, **move):
        return pltpu.make_async_remote_copy(
            src_ref=src, dst_ref=dst, send_sem=self.send.at[t, n], recv_sem=self.recv.at[t, n],
            device_id=device(self.spot, **move), device_id_type=MESH)

    def pair(self, t):
        return self.copy(t, 0, self.pair_out.at[t % 3], self.own.at[t], c=1)

    def parts(self, t, phase, axes):
        axis = axes[phase]
        me = self.spot[axis]
        fixed = {a: self.spot[a] for a in axes[:phase]}
        chunk = lambda by: {**fixed, axis: (me + by) % 4}
        second = (self.r2, self.s2, self.t2)[phase]
        n = 1 + 4 * phase
        mine = self.view(t, chunk(0))
        if phase:
            def copies(i):
                return self.copy(t, n + i, self.view(t, chunk(i + 1)), second.at[t, i], **{axis: i + 1})

            return copies, (None, None, mine), (None, second.at[t])
        rest = [a for a in "xzy" if a != axis][0]
        half = lambda by, k: self.view(t, {**chunk(by), rest: pl.ds(2 * k, 2)})

        def copies(i):
            src = (half(2, 0), half(2, 1), self.view(t, chunk(1)), self.view(t, chunk(3)))[i]
            dst = (self.r1, self.r1, second, second)[i].at[t, i % 2]
            return self.copy(t, n + i, src, dst, **{axis: 1 + 2 * (i % 2)})

        return copies, (half(1, 0), half(3, 1), mine), (self.r1.at[t], second.at[t])

    def partner_tile(self, t):
        pl.when(t >= 3)(lambda: self.pair(t - 3).wait_send())
        c = self.spot["c"]
        for xx in range(4):
            got = dot(self.lhs[xx, 1 - c], self.rhs[:, lanes(t, WIDE)])
            self.pair_out[t % 3, xx] = got.reshape(4, 4, 16, WIDE)
        self.pair(t).start()

    def own_tile(self, t):
        c = self.spot["c"]
        self.pair(t).wait_recv()
        for xx in range(4):
            got = dot(self.lhs[xx, c], self.rhs[:, lanes(t, WIDE)])
            self.own[t, xx] = self.own[t, xx] + got.reshape(4, 4, 16, WIDE)
        self.each(t, functools.partial(self.begin, t, 0))

    def begin(self, t, phase, axes):
        copies, _, _ = self.parts(t, phase, axes)
        for i in (1, 0, 2) if phase else (0, 1):
            copies(i).start()

    def pass_on(self, t):
        def body(axes):
            copies, (after, before, _), (first, _) = self.parts(t, 0, axes)
            copies(0).wait_recv()
            after[...] = after[...] + first[0]
            copies(2).start()
            copies(1).wait_recv()
            before[...] = before[...] + first[1]
            copies(3).start()

        self.each(t, body)

    def finish(self, t, phase):
        def body(axes):
            copies, (_, _, mine), (_, second) = self.parts(t, phase, axes)
            for i in range(3) if phase else (2, 3):
                copies(i).wait_recv()
            total = mine[...] + second[0] + second[1]
            if phase:
                total = total + second[2]
            if phase == 2:
                self.out[:, lanes(t, WIDE)] = total * self.scale
            else:
                mine[...] = total
                self.begin(t, phase + 1, axes)

        self.each(t, body)

    def drain(self):
        @pl.loop(0, TILES)
        def _(t):
            pl.when(t >= TILES - 3)(lambda: self.pair(t).wait_send())

            def body(axes):
                for phase in range(3):
                    for i in range(3 if phase else 4):
                        self.parts(t, phase, axes)[0](i).wait_send()

            self.each(t, body)

    @staticmethod
    def scratch():
        V = pltpu.VMEM
        return [
            V((TILES, 4, 4, 4, 16, WIDE), f32),
            V((3, 4, 4, 4, 16, WIDE), f32),
            V((TILES, 2, 2, 4, 16, WIDE), f32),
            V((TILES, 2, 4, 4, 16, WIDE), f32),
            V((TILES, 3, 4, 16, WIDE), f32),
            V((TILES, 3, 16, WIDE), f32),
            pltpu.SemaphoreType.DMA((TILES, 13)),
            pltpu.SemaphoreType.DMA((TILES, 13)),
        ]


FLOW = len(Flow.scratch())
SCATTER = len(Scatter.scratch())


def layer(scale, q_in, k_in, v_in, w_in, og_in, res_out, gq_out, gk_out, gv_out, gw_out, *refs):
    (q, k, v, og, g, att, gq, att_t, intra, wrow, wcol, col, tri, tri_t, ctri, ctri_t, crow,
     in_sem, row_sem, col_sem, out_sem) = refs[:21]
    pre_refs, suf_refs, sc_refs = refs[21:21 + FLOW], refs[21 + FLOW:21 + 2 * FLOW], refs[21 + 2 * FLOW:]
    spot = place()
    met = greet(spot)
    c = spot["c"]
    pre, suf = Flow(spot, pre_refs, False), Flow(spot, suf_refs, True)
    scatter = Scatter(spot, att_t, og, gw_out, sc_refs, scale)

    def load(n, src, dst, part):
        cols = pl.ds(pl.multiple_of(part * 1024, 1024), 1024)
        return pltpu.make_async_copy(src.at[:, cols], dst.at[:, cols], in_sem.at[n])

    theirs, ours = 1 - c, c
    loads = {}
    for n, (name, src, dst, part) in enumerate((
            ("k0", k_in, k, theirs), ("v0", v_in, v, theirs), ("k1", k_in, k, ours), ("v1", v_in, v, ours),
            ("q0", q_in, q, theirs), ("q1", q_in, q, ours), ("og0", og_in, og, theirs), ("og1", og_in, og, ours))):
        loads[name] = load(n, src, dst, part)

    def tile_of(p):
        return (p + 4 * theirs) % 8

    def row_tile(p):
        rows = pl.ds(pl.multiple_of(tile_of(p) * WIDE, WIDE), WIDE)
        return pltpu.make_async_copy(w_in.at[rows], wrow.at[p % 3], row_sem.at[p])

    def col_tile(n):
        return pltpu.make_async_copy(w_in.at[:, lanes(n, WIDE)], wcol.at[n % 2], col_sem.at[n])

    for name in ("k0", "v0", "k1", "v1", "q0", "q1"):
        loads[name].start()
    row_tile(0).start()
    loads["og0"].start()
    loads["og1"].start()
    row_tile(1).start()
    row_tile(2).start()

    base = lax.axis_index("seq") * TOK + 1

    def scale_of(shape, dim):
        index = lax.broadcasted_iota(jnp.int32, shape, dim)
        return lax.rsqrt((DH * (index + base)).astype(f32))

    col[...] = scale_of((TOK, DH), 0)
    crow[...] = scale_of((8, TOK), 1)
    below = (lax.broadcasted_iota(jnp.int32, (MID, MID), 0) >= lax.broadcasted_iota(jnp.int32, (MID, MID), 1)).astype(f32)
    above = (lax.broadcasted_iota(jnp.int32, (MID, MID), 0) <= lax.broadcasted_iota(jnp.int32, (MID, MID), 1)).astype(f32)
    tri[...] = below
    for b, rows in enumerate((A, B)):
        ctri[b] = jnp.concatenate([col[rows]] * 2, axis=1) * below
        ctri_t[b] = crow[0:1, rows] * above
    pre.clear()
    suf.clear()
    met()

    def local_state(h):
        pre.local[h] = dot(k[:, lanes(h)].T, v[:, lanes(h)])

    def local_grad(h):
        high, low = two(col[...] * q[:, lanes(h)].astype(f32))
        both = dot(g[:, lanes(h)].T, jnp.concatenate([high, low], axis=1))
        suf.local[h] = both[:, :DH] + both[:, DH:]

    def attend_intra(h):
        hs = lanes(h)
        c_b = jnp.concatenate([col[B]] * 2, axis=1)
        w_a = (dot_nt(q[A, hs], k[A, hs]) * ctri[0]).astype(bf16)
        w_ba = (dot_nt(q[B, hs], k[A, hs]) * c_b).astype(bf16)
        w_bb = (dot_nt(q[B, hs], k[B, hs]) * ctri[1]).astype(bf16)
        intra[h, A] = dot(w_a, v[A, hs])
        intra[h, B] = dot(jnp.concatenate([w_ba, w_bb], axis=1), v[:, hs])

    def attend(h):
        hs = lanes(h)
        high, low = two(pre.state[h])
        x = q[:, hs]
        inter = dot(jnp.concatenate([x, x], axis=1), jnp.concatenate([high, low], axis=0))
        got = (col[...] * inter + intra[h]).astype(bf16)
        att[:, hs] = got
        att_t[h // 4, h % 4 // 2, lanes(h % 2)] = got.T

    def grad_att(p):
        row_tile(p).wait()
        n = tile_of(p)
        g[:, lanes(n, WIDE)] = dot_nt(og[...], wrow[p % 3]).astype(bf16)
        pl.when(p + 3 < TILES)(lambda: row_tile(p + 3).start())

        @pl.loop(0, 2)
        def _(e):
            local_grad(2 * n + e)
            pl.when(p < 4)(lambda: suf.pair(2 * p + e).start())

    def back_q(h):
        hs = lanes(h)
        ga, gb, va, vb = (r[s, hs] for r in (g, v) for s in (A, B))
        gg = g[:, hs]
        r_a = (dot_nt(ga, va) * tri[...]).astype(bf16)
        r_ba = dot_nt(gb, va).astype(bf16)
        r_bb = (dot_nt(gb, vb) * tri[...]).astype(bf16)
        high, low = two(pre.state[h])
        inter = dot_nt(jnp.concatenate([gg, gg], axis=1), jnp.concatenate([high, low], axis=1))
        gq[A, hs] = (col[A] * (inter[:MID] + dot(r_a, k[A, hs]))).astype(bf16)
        gq[B, hs] = (col[B] * (inter[MID:] + dot(jnp.concatenate([r_ba, r_bb], axis=1), k[:, hs]))).astype(bf16)
        head_out(0, h).start()

    def back_kv(h):
        hs = lanes(h)
        ga, gb, va, vb, ka, kb, qa, qb = (r[s, hs] for r in (g, v, k, q) for s in (A, B))
        gg, vv, kk, qq = g[:, hs], v[:, hs], k[:, hs], q[:, hs]
        c_b = crow[0:1, B]
        high, low = two(suf.state[h])
        s_aa = (dot_nt(va, ga) * ctri_t[0]).astype(bf16)
        s_ab = (dot_nt(va, gb) * c_b).astype(bf16)
        s_bb = (dot_nt(vb, gb) * ctri_t[1]).astype(bf16)
        inter = dot(jnp.concatenate([vv, vv], axis=1), jnp.concatenate([high, low], axis=0))
        gk_a = (inter[:MID] + dot(jnp.concatenate([s_aa, s_ab], axis=1), qq)).astype(bf16)
        gk_b = (inter[MID:] + dot(s_bb, qb)).astype(bf16)
        w_aa = (dot_nt(ka, qa) * ctri_t[0]).astype(bf16)
        w_ab = (dot_nt(ka, qb) * c_b).astype(bf16)
        w_bb = (dot_nt(kb, qb) * ctri_t[1]).astype(bf16)
        inter = dot_nt(jnp.concatenate([kk, kk], axis=1), jnp.concatenate([high, low], axis=1))
        gv_a = (inter[:MID] + dot(jnp.concatenate([w_aa, w_ab], axis=1), gg)).astype(bf16)
        gv_b = (inter[MID:] + dot(w_bb, gb)).astype(bf16)
        k[A, hs], k[B, hs] = gk_a, gk_b
        v[A, hs], v[B, hs] = gv_a, gv_b
        for n in (1, 2):
            head_out(n, h).start()

    def head_out(n, h):
        src, dst = ((gq, gq_out), (k, gk_out), (v, gv_out))[n]
        return pltpu.make_async_copy(src.at[:, lanes(h)], dst.at[:, lanes(h)], out_sem.at[n, h])

    def result_out(n):
        return pltpu.make_async_copy(og.at[:, lanes(n, WIDE)], res_out.at[:, lanes(n, WIDE)], out_sem.at[3, n])

    def result(n):
        col_tile(n).wait()
        og[:, lanes(n, WIDE)] = dot(att[...], wcol[n % 2]).astype(bf16)
        result_out(n).start()
        pl.when(n + 2 < TILES)(lambda: col_tile(n + 2).start())

    loads["k0"].wait()
    loads["v0"].wait()
    @pl.loop(0, HALF)
    def _(i):
        local_state(HALF * theirs + i)
        pre.pair(i).start()

    loads["k1"].wait()
    loads["v1"].wait()

    @pl.loop(0, HALF)
    def _(i):
        local_state(HALF * ours + i)
        pl.when(pre.rank == 0)(lambda: pre.step(i))

    for name in ("q0", "q1"):
        loads[name].wait()

    def attend_pair(i, _):
        attend(HALF * c + i)
        pre.share(i).wait_recv()
        attend(HALF * (1 - c) + i)

    def attended(p):
        return jnp.minimum(pre.due(p - 2, -3), jnp.minimum(p // 2, HALF))

    col_tile(0).start()
    col_tile(1).start()
    def attend_due(p):
        lax.fori_loop(attended(p), attended(p + 1), attend_pair, None)

    loads["og0"].wait()
    loads["og1"].wait()

    @pl.loop(0, TILES)
    def _(n):
        pre.steps(2 * n, -1)

        @pl.loop(0, 2)
        def _(e):
            attend_intra(HALF * e + n)

        attend_due(2 * n)
        pre.steps(2 * n + 1, -1)
        grad_att(n)
        attend_due(2 * n + 1)

    suf.steps(0)

    @pl.loop(2 * TILES, 2 * TILES + HALF)
    def _(p):
        pre.steps(p, -1)
        attend_due(p)

        @pl.loop(0, 2)
        def _(e):
            back_q(HALF * ((c + e) % 2) + p - 2 * TILES)

    @pl.loop(0, TILES + 2)
    def _(n):
        pl.when(n < TILES)(lambda: scatter.partner_tile(n))
        pl.when(n >= 2)(lambda: scatter.own_tile(n - 2))
        suf.steps(n + 1)

    @pl.loop(0, TILES)
    def _(n):
        scatter.pass_on(n)
        result(n)
        suf.steps(TILES + 3 + n)

    suf.steps(2 * TILES + 3)
    suf.steps(2 * TILES + 4)

    @pl.loop(0, TILES)
    def _(n):
        scatter.finish(n, 0)

        @pl.loop(0, 2)
        def _(e):
            pl.when(e == 1)(lambda: suf.share(n).wait_recv())
            back_kv(HALF * ((c + e) % 2) + n)

    for phase in (1, 2):
        pl.loop(0, TILES)(lambda n: scatter.finish(n, phase))
    scatter.drain()
    pre.drain()
    suf.drain()
    @pl.loop(0, HEADS)
    def _(h):
        for n in range(3):
            head_out(n, h).wait()

    pl.loop(0, TILES)(lambda n: result_out(n).wait())


def local(queries, keys, values, out_weight, out_grad):
    tokens = lax.axis_size("dp") * lax.axis_size("seq") * TOK
    wide = lambda: pltpu.VMEM((TOK, HD), bf16)
    hbm = pl.BlockSpec(memory_space=pl.ANY)
    rows = jax.ShapeDtypeStruct((TOK, HD), bf16)
    sem = pltpu.SemaphoreType.DMA
    outs = pl.pallas_call(
        functools.partial(layer, float(tokens) ** -0.5),
        out_shape=[rows] * 4 + [jax.ShapeDtypeStruct((16, HD), f32)],
        in_specs=[hbm] * 5,
        out_specs=[hbm] * 4 + [pl.BlockSpec(memory_space=pltpu.VMEM)],
        scratch_shapes=[
            wide(), wide(), wide(), wide(), wide(), wide(), wide(),
            pltpu.VMEM((4, 2, 256, TOK), bf16),
            pltpu.VMEM((HEADS, TOK, DH), f32),
            pltpu.VMEM((3, WIDE, HD), bf16),
            pltpu.VMEM((2, HD, WIDE), bf16),
            pltpu.VMEM((TOK, DH), f32),
            pltpu.VMEM((MID, MID), f32),
            pltpu.VMEM((MID, MID), f32),
            pltpu.VMEM((2, MID, MID), f32),
            pltpu.VMEM((2, MID, MID), f32),
            pltpu.VMEM((8, TOK), f32),
            sem((8,)), sem((TILES,)), sem((TILES,)), sem((4, HEADS)),
        ] + Flow.scratch() + Flow.scratch() + Scatter.scratch(),
        compiler_params=pltpu.CompilerParams(collective_id=0, has_side_effects=True, vmem_limit_bytes=60 * 2**20),
        cost_estimate=pl.CostEstimate(flops=23 * 10**9, bytes_accessed=25 * 10**6, transcendentals=0),
    )(*(x.reshape(TOK, HD) for x in (queries, keys, values)), out_weight, out_grad.reshape(TOK, HD))
    return tuple(x if x.shape[0] == 16 else x.reshape(1, TOK, HD) for x in put(outs))


def put_kernel(*refs):
    ins, outs, held, sem = refs[:5], refs[5:10], refs[10:15], refs[15]
    parts = []
    for n in range(5):
        step = ins[n].shape[0] // 2
        for part in range(2):
            rows = pl.ds(part * step, step)
            parts.append((
                pltpu.make_async_copy(ins[n].at[rows], held[n].at[rows], sem.at[0, n, part]),
                pltpu.make_async_copy(held[n].at[rows], outs[n].at[rows], sem.at[1, n, part])))
    for get, _ in parts:
        get.start()
    for get, give in parts:
        get.wait()
        give.start()
    for _, give in parts:
        give.wait()


def put(arrays):
    hbm = pl.BlockSpec(memory_space=pl.ANY)
    return pl.pallas_call(
        put_kernel,
        out_shape=[jax.ShapeDtypeStruct(x.shape, x.dtype) for x in arrays],
        in_specs=[hbm] * 5,
        out_specs=[hbm] * 5,
        scratch_shapes=[pltpu.VMEM(x.shape, x.dtype) for x in arrays] + [pltpu.SemaphoreType.DMA((2, 5, 2))],
        compiler_params=pltpu.CompilerParams(vmem_limit_bytes=60 * 2**20),
    )(*arrays)


def solution(mesh):
    in_specs = (
        P("dp", "seq", None),
        P("dp", "seq", None),
        P("dp", "seq", None),
        P(),
        P("dp", "seq", None),
    )
    out_specs = (
        P("dp", "seq", None),
        P("dp", "seq", None),
        P("dp", "seq", None),
        P("dp", "seq", None),
        P(("seq", "dp"), None),
    )
    return jax.shard_map(local, mesh=mesh, in_specs=in_specs, out_specs=out_specs, check_vma=False)
```

```python
import functools

import jax
import jax.numpy as jnp
from jax import lax
from jax.experimental import pallas as pl
from jax.experimental.pallas import tpu as pltpu
from jax.sharding import PartitionSpec as P

MESH = pl.DeviceIdType.MESH
HEADS = 16
HALF = 8
DH = 128
TOK = 512
MID = 256
HD = 2048
TILES = 8
WIDE = 256
LAG = 2
Y_FIRST, Z_FIRST, X_FIRST = ("y", "z", "x"), ("z", "x", "y"), ("x", "y", "z")
ORDERS = (Y_FIRST, Z_FIRST, X_FIRST)
ALL = slice(None)
A, B = pl.ds(0, MID), pl.ds(MID, MID)
f32, bf16 = jnp.float32, jnp.bfloat16


def place():
    s, d = lax.axis_index("seq"), lax.axis_index("dp")
    return {"x": s // 2, "c": s % 2, "z": d // 4, "y": d % 4}


def device(spot, **moves):
    spot = dict(spot)
    for axis, by in moves.items():
        spot[axis] = (spot[axis] + by) % (2 if axis == "c" else 4)
    return (spot["x"] * 2 + spot["c"], spot["z"] * 4 + spot["y"])


def greet(spot):
    barrier = pltpu.get_barrier_semaphore()
    partners = [device(spot, c=1)]
    for axis in "xyz":
        partners += [device(spot, **{axis: by}) for by in (1, 2, 3)]
    for partner in partners:
        pl.semaphore_signal(barrier, 1, device_id=partner, device_id_type=MESH)
    return lambda: pl.semaphore_wait(barrier, len(partners))


def dot(a, b):
    return jnp.dot(a, b, preferred_element_type=f32)


def dot_nt(a, b):
    return lax.dot_general(a, b, (((1,), (1,)), ((), ())), preferred_element_type=f32)


def lanes(h, size=DH):
    return pl.ds(h * size if isinstance(h, int) else pl.multiple_of(h * size, size), size)


def two(value):
    high = value.astype(bf16)
    return high, (value - high.astype(f32)).astype(bf16)


class Flow:
    def __init__(self, spot, refs, backward):
        self.local, self.pair_in, self.chain_in, self.chain_out, self.share_out, self.state, self.send, self.recv = refs
        self.spot, self.c = spot, spot["c"]
        self.rank = 3 - spot["x"] if backward else spot["x"]
        self.move = 3 if backward else 1
        self.first = (self.c == (1 if backward else 0)).astype(f32)

    @staticmethod
    def scratch():
        full, half = pltpu.VMEM((HEADS, DH, DH), f32), pltpu.VMEM((HALF, DH, DH), f32)
        sems = pltpu.SemaphoreType.DMA((3, HALF))
        return [full, half, half, half, half, full, sems, sems]

    def copy(self, kind, i, src, dst, **move):
        return pltpu.make_async_remote_copy(
            src_ref=src, dst_ref=dst, send_sem=self.send.at[kind, i], recv_sem=self.recv.at[kind, i],
            device_id=device(self.spot, **move), device_id_type=MESH)

    def pair(self, i):
        return self.copy(0, i, self.local.at[HALF * (1 - self.c) + i], self.pair_in.at[i], c=1)

    def chain(self, i):
        return self.copy(1, i, self.chain_out.at[i], self.chain_in.at[i], x=self.move)

    def share(self, i):
        return self.copy(2, i, self.share_out.at[i], self.state.at[HALF * self.c + i], c=1)

    def clear(self):
        @pl.when(self.rank == 0)
        def _():
            self.chain_in[...] = jnp.zeros_like(self.chain_in)

    def step(self, i):
        mine = HALF * self.c + i
        self.pair(i).wait_recv()

        @pl.when(self.rank > 0)
        def _():
            self.chain(i).wait_recv()

        @pl.when(self.rank < 3)
        def _():
            self.chain_out[i] = self.chain_in[i] + (self.local[mine] + self.pair_in[i])
            self.chain(i).start()

        self.share_out[i] = self.chain_in[i] + self.first * self.local[mine]
        self.share(i).start()
        self.state[mine] = self.chain_in[i] + (1.0 - self.first) * self.pair_in[i]

    def due(self, p, start=0):
        late = jnp.maximum(p - 3 * self.rank, 0)
        return jnp.where(self.rank == 0, jnp.where(p <= start, 0, HALF), jnp.minimum((2 * late + 2) // 3, HALF))

    def steps(self, p, start=0, slots=1):
        lax.fori_loop(self.due(p, start), self.due(p + slots, start), lambda i, _: self.step(i), None)

    def drain(self):
        @pl.loop(0, HALF)
        def _(i):
            self.pair(i).wait_send()
            self.share(i).wait_send()

            @pl.when(self.rank < 3)
            def _():
                self.chain(i).wait_send()


class Scatter:
    def __init__(self, spot, lhs, rhs, out, refs, scale):
        (self.own, self.pair_out, self.r1, self.r2, self.s2,
         self.t2, self.send, self.recv) = refs
        self.spot, self.lhs, self.rhs, self.out, self.scale = spot, lhs, rhs, out, scale

    def each(self, t, body):
        kind = jnp.where(t < 6, t % 2, 2)
        for n, axes in enumerate(ORDERS):
            pl.when(kind == n)(functools.partial(body, axes))

    def view(self, t, sel, rows=ALL):
        return self.own.at[t, sel.get("x", ALL), sel.get("z", ALL), sel.get("y", ALL), rows]

    def copy(self, t, n, src, dst, **move):
        return pltpu.make_async_remote_copy(
            src_ref=src, dst_ref=dst, send_sem=self.send.at[t, n], recv_sem=self.recv.at[t, n],
            device_id=device(self.spot, **move), device_id_type=MESH)

    def pair(self, t):
        return self.copy(t, 0, self.pair_out.at[t % 3], self.own.at[t], c=1)

    def parts(self, t, phase, axes):
        axis = axes[phase]
        me = self.spot[axis]
        fixed = {a: self.spot[a] for a in axes[:phase]}
        chunk = lambda by: {**fixed, axis: (me + by) % 4}
        second = (self.r2, self.s2, self.t2)[phase]
        n = 1 + 4 * phase
        mine = self.view(t, chunk(0))
        if phase:
            def copies(i):
                return self.copy(t, n + i, self.view(t, chunk(i + 1)), second.at[t, i], **{axis: i + 1})

            return copies, (None, None, mine), (None, second.at[t])
        rest = [a for a in "xzy" if a != axis][0]
        half = lambda by, k: self.view(t, {**chunk(by), rest: pl.ds(2 * k, 2)})

        def copies(i):
            src = (half(2, 0), half(2, 1), self.view(t, chunk(1)), self.view(t, chunk(3)))[i]
            dst = (self.r1, self.r1, second, second)[i].at[t, i % 2]
            return self.copy(t, n + i, src, dst, **{axis: 1 + 2 * (i % 2)})

        return copies, (half(1, 0), half(3, 1), mine), (self.r1.at[t], second.at[t])

    def partner_tile(self, t):
        pl.when(t >= 3)(lambda: self.pair(t - 3).wait_send())
        c = self.spot["c"]
        for xx in range(4):
            got = dot(self.lhs[xx, 1 - c], self.rhs[:, lanes(t, WIDE)])
            self.pair_out[t % 3, xx] = got.reshape(4, 4, 16, WIDE)
        self.pair(t).start()

    def own_tile(self, t):
        c = self.spot["c"]
        self.pair(t).wait_recv()
        for xx in range(4):
            got = dot(self.lhs[xx, c], self.rhs[:, lanes(t, WIDE)])
            self.own[t, xx] = self.own[t, xx] + got.reshape(4, 4, 16, WIDE)
        self.each(t, functools.partial(self.begin, t, 0))

    def begin(self, t, phase, axes):
        copies, _, _ = self.parts(t, phase, axes)
        for i in (1, 0, 2) if phase else (0, 1):
            copies(i).start()

    def pass_on(self, t):
        def body(axes):
            copies, (after, before, _), (first, _) = self.parts(t, 0, axes)
            copies(0).wait_recv()
            after[...] = after[...] + first[0]
            copies(2).start()
            copies(1).wait_recv()
            before[...] = before[...] + first[1]
            copies(3).start()

        self.each(t, body)

    def finish(self, t, phase):
        def body(axes):
            copies, (_, _, mine), (_, second) = self.parts(t, phase, axes)
            for i in range(3) if phase else (2, 3):
                copies(i).wait_recv()
            total = mine[...] + second[0] + second[1]
            if phase:
                total = total + second[2]
            if phase == 2:
                self.out[:, lanes(t, WIDE)] = total * self.scale
            else:
                mine[...] = total
                self.begin(t, phase + 1, axes)

        self.each(t, body)

    def drain(self):
        @pl.loop(0, TILES)
        def _(t):
            pl.when(t >= TILES - 3)(lambda: self.pair(t).wait_send())

            def body(axes):
                for phase in range(3):
                    for i in range(3 if phase else 4):
                        self.parts(t, phase, axes)[0](i).wait_send()

            self.each(t, body)

    @staticmethod
    def scratch():
        V = pltpu.VMEM
        return [
            V((TILES, 4, 4, 4, 16, WIDE), f32),
            V((3, 4, 4, 4, 16, WIDE), f32),
            V((TILES, 2, 2, 4, 16, WIDE), f32),
            V((TILES, 2, 4, 4, 16, WIDE), f32),
            V((TILES, 3, 4, 16, WIDE), f32),
            V((TILES, 3, 16, WIDE), f32),
            pltpu.SemaphoreType.DMA((TILES, 13)),
            pltpu.SemaphoreType.DMA((TILES, 13)),
        ]


FLOW = len(Flow.scratch())
SCATTER = len(Scatter.scratch())


def layer(scale, q_in, k_in, v_in, w_in, og_in, res_out, gq_out, gk_out, gv_out, gw_out, *refs):
    (q, k, v, og, g, att, gq, att_t, intra, wrow, wcol, col, tri, tri_t, ctri, ctri_t, crow,
     in_sem, row_sem, col_sem, out_sem) = refs[:21]
    pre_refs, suf_refs, sc_refs = refs[21:21 + FLOW], refs[21 + FLOW:21 + 2 * FLOW], refs[21 + 2 * FLOW:]
    spot = place()
    met = greet(spot)
    c = spot["c"]
    pre, suf = Flow(spot, pre_refs, False), Flow(spot, suf_refs, True)
    scatter = Scatter(spot, att_t, og, gw_out, sc_refs, scale)

    def load(n, src, dst, part):
        cols = pl.ds(pl.multiple_of(part * 1024, 1024), 1024)
        return pltpu.make_async_copy(src.at[:, cols], dst.at[:, cols], in_sem.at[n])

    theirs, ours = 1 - c, c
    loads = {}
    for n, (name, src, dst, part) in enumerate((
            ("k0", k_in, k, theirs), ("v0", v_in, v, theirs), ("k1", k_in, k, ours), ("v1", v_in, v, ours),
            ("q0", q_in, q, theirs), ("q1", q_in, q, ours), ("og0", og_in, og, theirs), ("og1", og_in, og, ours))):
        loads[name] = load(n, src, dst, part)

    def tile_of(p):
        return (p + 4 * theirs) % 8

    def row_tile(p):
        rows = pl.ds(pl.multiple_of(tile_of(p) * WIDE, WIDE), WIDE)
        return pltpu.make_async_copy(w_in.at[rows], wrow.at[p % 3], row_sem.at[p])

    def col_tile(n):
        return pltpu.make_async_copy(w_in.at[:, lanes(n, WIDE)], wcol.at[n % 2], col_sem.at[n])

    for name in ("k0", "v0", "k1", "v1", "q0", "q1"):
        loads[name].start()
    row_tile(0).start()
    loads["og0"].start()
    loads["og1"].start()
    row_tile(1).start()
    row_tile(2).start()

    base = lax.axis_index("seq") * TOK + 1

    def scale_of(shape, dim):
        index = lax.broadcasted_iota(jnp.int32, shape, dim)
        return lax.rsqrt((DH * (index + base)).astype(f32))

    col[...] = scale_of((TOK, DH), 0)
    crow[...] = scale_of((8, TOK), 1)
    below = (lax.broadcasted_iota(jnp.int32, (MID, MID), 0) >= lax.broadcasted_iota(jnp.int32, (MID, MID), 1)).astype(f32)
    above = (lax.broadcasted_iota(jnp.int32, (MID, MID), 0) <= lax.broadcasted_iota(jnp.int32, (MID, MID), 1)).astype(f32)
    tri[...] = below
    for b, rows in enumerate((A, B)):
        ctri[b] = jnp.concatenate([col[rows]] * 2, axis=1) * below
        ctri_t[b] = crow[0:1, rows] * above
    pre.clear()
    suf.clear()
    met()

    def local_state(h):
        pre.local[h] = dot(k[:, lanes(h)].T, v[:, lanes(h)])

    def local_grad(h):
        high, low = two(col[...] * q[:, lanes(h)].astype(f32))
        both = dot(g[:, lanes(h)].T, jnp.concatenate([high, low], axis=1))
        suf.local[h] = both[:, :DH] + both[:, DH:]

    def attend_intra(h):
        hs = lanes(h)
        c_b = jnp.concatenate([col[B]] * 2, axis=1)
        w_a = (dot_nt(q[A, hs], k[A, hs]) * ctri[0]).astype(bf16)
        w_ba = (dot_nt(q[B, hs], k[A, hs]) * c_b).astype(bf16)
        w_bb = (dot_nt(q[B, hs], k[B, hs]) * ctri[1]).astype(bf16)
        intra[h, A] = dot(w_a, v[A, hs])
        intra[h, B] = dot(jnp.concatenate([w_ba, w_bb], axis=1), v[:, hs])

    def attend(h):
        hs = lanes(h)
        high, low = two(pre.state[h])
        x = q[:, hs]
        inter = dot(jnp.concatenate([x, x], axis=1), jnp.concatenate([high, low], axis=0))
        got = (col[...] * inter + intra[h]).astype(bf16)
        att[:, hs] = got
        att_t[h // 4, h % 4 // 2, lanes(h % 2)] = got.T

    def grad_att(p):
        row_tile(p).wait()
        n = tile_of(p)
        g[:, lanes(n, WIDE)] = dot_nt(og[...], wrow[p % 3]).astype(bf16)
        pl.when(p + 3 < TILES)(lambda: row_tile(p + 3).start())

        @pl.loop(0, 2)
        def _(e):
            local_grad(2 * n + e)
            pl.when(p < 4)(lambda: suf.pair(2 * p + e).start())

    def back_q(h):
        hs = lanes(h)
        ga, gb, va, vb = (r[s, hs] for r in (g, v) for s in (A, B))
        gg = g[:, hs]
        r_a = (dot_nt(ga, va) * tri[...]).astype(bf16)
        r_ba = dot_nt(gb, va).astype(bf16)
        r_bb = (dot_nt(gb, vb) * tri[...]).astype(bf16)
        high, low = two(pre.state[h])
        inter = dot_nt(jnp.concatenate([gg, gg], axis=1), jnp.concatenate([high, low], axis=1))
        gq[A, hs] = (col[A] * (inter[:MID] + dot(r_a, k[A, hs]))).astype(bf16)
        gq[B, hs] = (col[B] * (inter[MID:] + dot(jnp.concatenate([r_ba, r_bb], axis=1), k[:, hs]))).astype(bf16)
        head_out(0, h).start()

    def back_kv(h):
        hs = lanes(h)
        ga, gb, va, vb, ka, kb, qa, qb = (r[s, hs] for r in (g, v, k, q) for s in (A, B))
        gg, vv, kk, qq = g[:, hs], v[:, hs], k[:, hs], q[:, hs]
        c_b = crow[0:1, B]
        high, low = two(suf.state[h])
        s_aa = (dot_nt(va, ga) * ctri_t[0]).astype(bf16)
        s_ab = (dot_nt(va, gb) * c_b).astype(bf16)
        s_bb = (dot_nt(vb, gb) * ctri_t[1]).astype(bf16)
        inter = dot(jnp.concatenate([vv, vv], axis=1), jnp.concatenate([high, low], axis=0))
        gk_a = (inter[:MID] + dot(jnp.concatenate([s_aa, s_ab], axis=1), qq)).astype(bf16)
        gk_b = (inter[MID:] + dot(s_bb, qb)).astype(bf16)
        w_aa = (dot_nt(ka, qa) * ctri_t[0]).astype(bf16)
        w_ab = (dot_nt(ka, qb) * c_b).astype(bf16)
        w_bb = (dot_nt(kb, qb) * ctri_t[1]).astype(bf16)
        inter = dot_nt(jnp.concatenate([kk, kk], axis=1), jnp.concatenate([high, low], axis=1))
        gv_a = (inter[:MID] + dot(jnp.concatenate([w_aa, w_ab], axis=1), gg)).astype(bf16)
        gv_b = (inter[MID:] + dot(w_bb, gb)).astype(bf16)
        k[A, hs], k[B, hs] = gk_a, gk_b
        v[A, hs], v[B, hs] = gv_a, gv_b
        for n in (1, 2):
            head_out(n, h).start()

    def head_out(n, h):
        src, dst = ((gq, gq_out), (k, gk_out), (v, gv_out))[n]
        return pltpu.make_async_copy(src.at[:, lanes(h)], dst.at[:, lanes(h)], out_sem.at[n, h])

    def result_out(n):
        return pltpu.make_async_copy(og.at[:, lanes(n, WIDE)], res_out.at[:, lanes(n, WIDE)], out_sem.at[3, n])

    def result(n):
        col_tile(n).wait()
        og[:, lanes(n, WIDE)] = dot(att[...], wcol[n % 2]).astype(bf16)
        result_out(n).start()
        pl.when(n + 2 < TILES)(lambda: col_tile(n + 2).start())

    loads["k0"].wait()
    loads["v0"].wait()
    @pl.loop(0, HALF)
    def _(i):
        local_state(HALF * theirs + i)
        pre.pair(i).start()

    loads["k1"].wait()
    loads["v1"].wait()

    @pl.loop(0, HALF)
    def _(i):
        local_state(HALF * ours + i)
        pl.when(pre.rank == 0)(lambda: pre.step(i))

    for name in ("q0", "q1"):
        loads[name].wait()

    def attend_pair(i, _):
        attend(HALF * c + i)
        pre.share(i).wait_recv()
        attend(HALF * (1 - c) + i)

    def attended(p):
        return jnp.minimum(pre.due(p - 2, -3), jnp.minimum(p // 2, HALF))

    col_tile(0).start()
    col_tile(1).start()
    def attend_due(p):
        lax.fori_loop(attended(p), attended(p + 1), attend_pair, None)

    loads["og0"].wait()
    loads["og1"].wait()

    @pl.loop(0, TILES)
    def _(n):
        pre.steps(2 * n, -1)

        @pl.loop(0, 2)
        def _(e):
            attend_intra(HALF * e + n)

        attend_due(2 * n)
        pre.steps(2 * n + 1, -1)
        grad_att(n)
        attend_due(2 * n + 1)

    suf.steps(0)

    @pl.loop(2 * TILES, 2 * TILES + HALF)
    def _(p):
        pre.steps(p, -1)
        attend_due(p)
        pl.when(p % 2 == 1)(lambda: suf.steps((p - 15) // 2))

    @pl.loop(0, TILES + 2)
    def _(n):
        pl.when(n < TILES)(lambda: scatter.partner_tile(n))
        pl.when(n >= 2)(lambda: scatter.own_tile(n - 2))
        first = 5 + 16 * n // 10
        suf.steps(first, slots=5 + 16 * (n + 1) // 10 - first)

    @pl.loop(0, TILES)
    def _(n):
        scatter.pass_on(n)
        result(n)

    @pl.loop(0, TILES)
    def _(n):
        scatter.finish(n, 0)

        @pl.loop(0, 2)
        def _(e):
            pl.when(e == 1)(lambda: suf.share(n).wait_recv())
            back_q(HALF * ((c + e) % 2) + n)
            back_kv(HALF * ((c + e) % 2) + n)

    for phase in (1, 2):
        pl.loop(0, TILES)(lambda n: scatter.finish(n, phase))
    scatter.drain()
    pre.drain()
    suf.drain()
    @pl.loop(0, HEADS)
    def _(h):
        for n in range(3):
            head_out(n, h).wait()

    pl.loop(0, TILES)(lambda n: result_out(n).wait())


def local(queries, keys, values, out_weight, out_grad):
    tokens = lax.axis_size("dp") * lax.axis_size("seq") * TOK
    wide = lambda: pltpu.VMEM((TOK, HD), bf16)
    hbm = pl.BlockSpec(memory_space=pl.ANY)
    rows = jax.ShapeDtypeStruct((TOK, HD), bf16)
    sem = pltpu.SemaphoreType.DMA
    outs = pl.pallas_call(
        functools.partial(layer, float(tokens) ** -0.5),
        out_shape=[rows] * 4 + [jax.ShapeDtypeStruct((16, HD), f32)],
        in_specs=[hbm] * 5,
        out_specs=[hbm] * 4 + [pl.BlockSpec(memory_space=pltpu.VMEM)],
        scratch_shapes=[
            wide(), wide(), wide(), wide(), wide(), wide(), wide(),
            pltpu.VMEM((4, 2, 256, TOK), bf16),
            pltpu.VMEM((HEADS, TOK, DH), f32),
            pltpu.VMEM((3, WIDE, HD), bf16),
            pltpu.VMEM((2, HD, WIDE), bf16),
            pltpu.VMEM((TOK, DH), f32),
            pltpu.VMEM((MID, MID), f32),
            pltpu.VMEM((MID, MID), f32),
            pltpu.VMEM((2, MID, MID), f32),
            pltpu.VMEM((2, MID, MID), f32),
            pltpu.VMEM((8, TOK), f32),
            sem((8,)), sem((TILES,)), sem((TILES,)), sem((4, HEADS)),
        ] + Flow.scratch() + Flow.scratch() + Scatter.scratch(),
        compiler_params=pltpu.CompilerParams(collective_id=0, has_side_effects=True, vmem_limit_bytes=60 * 2**20),
        cost_estimate=pl.CostEstimate(flops=23 * 10**9, bytes_accessed=25 * 10**6, transcendentals=0),
    )(*(x.reshape(TOK, HD) for x in (queries, keys, values)), out_weight, out_grad.reshape(TOK, HD))
    return tuple(x if x.shape[0] == 16 else x.reshape(1, TOK, HD) for x in put(outs))


def put_kernel(*refs):
    ins, outs, held, sem = refs[:5], refs[5:10], refs[10:15], refs[15]
    parts = []
    for n in range(5):
        step = ins[n].shape[0] // 2
        for part in range(2):
            rows = pl.ds(part * step, step)
            parts.append((
                pltpu.make_async_copy(ins[n].at[rows], held[n].at[rows], sem.at[0, n, part]),
                pltpu.make_async_copy(held[n].at[rows], outs[n].at[rows], sem.at[1, n, part])))
    for get, _ in parts:
        get.start()
    for get, give in parts:
        get.wait()
        give.start()
    for _, give in parts:
        give.wait()


def put(arrays):
    hbm = pl.BlockSpec(memory_space=pl.ANY)
    return pl.pallas_call(
        put_kernel,
        out_shape=[jax.ShapeDtypeStruct(x.shape, x.dtype) for x in arrays],
        in_specs=[hbm] * 5,
        out_specs=[hbm] * 5,
        scratch_shapes=[pltpu.VMEM(x.shape, x.dtype) for x in arrays] + [pltpu.SemaphoreType.DMA((2, 5, 2))],
        compiler_params=pltpu.CompilerParams(vmem_limit_bytes=60 * 2**20),
    )(*arrays)


def solution(mesh):
    in_specs = (
        P("dp", "seq", None),
        P("dp", "seq", None),
        P("dp", "seq", None),
        P(),
        P("dp", "seq", None),
    )
    out_specs = (
        P("dp", "seq", None),
        P("dp", "seq", None),
        P("dp", "seq", None),
        P("dp", "seq", None),
        P(("seq", "dp"), None),
    )
    return jax.shard_map(local, mesh=mesh, in_specs=in_specs, out_specs=out_specs, check_vma=False)
```

```python
import functools

import jax
import jax.numpy as jnp
from jax import lax
from jax.experimental import pallas as pl
from jax.experimental.pallas import tpu as pltpu
from jax.sharding import PartitionSpec as P

MESH = pl.DeviceIdType.MESH
HEADS = 16
HALF = 8
DH = 128
TOK = 512
MID = 256
HD = 2048
TILES = 8
WIDE = 256
LAG = 2
Y_FIRST, Z_FIRST, X_FIRST = ("y", "z", "x"), ("z", "x", "y"), ("x", "y", "z")
ORDERS = (Y_FIRST, Z_FIRST, X_FIRST)
ALL = slice(None)
A, B = pl.ds(0, MID), pl.ds(MID, MID)
f32, bf16 = jnp.float32, jnp.bfloat16


def place():
    s, d = lax.axis_index("seq"), lax.axis_index("dp")
    return {"x": s // 2, "c": s % 2, "z": d // 4, "y": d % 4}


def device(spot, **moves):
    spot = dict(spot)
    for axis, by in moves.items():
        spot[axis] = (spot[axis] + by) % (2 if axis == "c" else 4)
    return (spot["x"] * 2 + spot["c"], spot["z"] * 4 + spot["y"])


def greet(spot):
    barrier = pltpu.get_barrier_semaphore()
    partners = [device(spot, c=1)]
    for axis in "xyz":
        partners += [device(spot, **{axis: by}) for by in (1, 2, 3)]
    for partner in partners:
        pl.semaphore_signal(barrier, 1, device_id=partner, device_id_type=MESH)
    return lambda: pl.semaphore_wait(barrier, len(partners))


def dot(a, b):
    return jnp.dot(a, b, preferred_element_type=f32)


def dot_nt(a, b):
    return lax.dot_general(a, b, (((1,), (1,)), ((), ())), preferred_element_type=f32)


def lanes(h, size=DH):
    return pl.ds(h * size if isinstance(h, int) else pl.multiple_of(h * size, size), size)


def two(value):
    high = value.astype(bf16)
    return high, (value - high.astype(f32)).astype(bf16)


class Flow:
    def __init__(self, spot, refs, backward):
        self.local, self.pair_in, self.chain_in, self.chain_out, self.share_out, self.state, self.send, self.recv = refs
        self.spot, self.c = spot, spot["c"]
        self.rank = 3 - spot["x"] if backward else spot["x"]
        self.move = 3 if backward else 1
        self.first = (self.c == (1 if backward else 0)).astype(f32)

    @staticmethod
    def scratch():
        full, half = pltpu.VMEM((HEADS, DH, DH), f32), pltpu.VMEM((HALF, DH, DH), f32)
        sems = pltpu.SemaphoreType.DMA((3, HALF))
        return [full, half, half, half, half, full, sems, sems]

    def copy(self, kind, i, src, dst, **move):
        return pltpu.make_async_remote_copy(
            src_ref=src, dst_ref=dst, send_sem=self.send.at[kind, i], recv_sem=self.recv.at[kind, i],
            device_id=device(self.spot, **move), device_id_type=MESH)

    def pair(self, i):
        return self.copy(0, i, self.local.at[HALF * (1 - self.c) + i], self.pair_in.at[i], c=1)

    def chain(self, i):
        return self.copy(1, i, self.chain_out.at[i], self.chain_in.at[i], x=self.move)

    def share(self, i):
        return self.copy(2, i, self.share_out.at[i], self.state.at[HALF * self.c + i], c=1)

    def clear(self):
        @pl.when(self.rank == 0)
        def _():
            self.chain_in[...] = jnp.zeros_like(self.chain_in)

    def step(self, i):
        mine = HALF * self.c + i
        self.pair(i).wait_recv()

        @pl.when(self.rank > 0)
        def _():
            self.chain(i).wait_recv()

        @pl.when(self.rank < 3)
        def _():
            self.chain_out[i] = self.chain_in[i] + (self.local[mine] + self.pair_in[i])
            self.chain(i).start()

        self.share_out[i] = self.chain_in[i] + self.first * self.local[mine]
        self.share(i).start()
        self.state[mine] = self.chain_in[i] + (1.0 - self.first) * self.pair_in[i]

    def due(self, p, start=0):
        late = jnp.maximum(p - 3 * self.rank, 0)
        return jnp.where(self.rank == 0, jnp.where(p <= start, 0, HALF), jnp.minimum((2 * late + 2) // 3, HALF))

    def steps(self, p, start=0, slots=1):
        lax.fori_loop(self.due(p, start), self.due(p + slots, start), lambda i, _: self.step(i), None)

    def drain(self):
        @pl.loop(0, HALF)
        def _(i):
            self.pair(i).wait_send()
            self.share(i).wait_send()

            @pl.when(self.rank < 3)
            def _():
                self.chain(i).wait_send()


class Scatter:
    def __init__(self, spot, lhs, rhs, out, refs, scale):
        (self.own, self.pair_out, self.r1, self.r2, self.s2,
         self.t2, self.send, self.recv) = refs
        self.spot, self.lhs, self.rhs, self.out, self.scale = spot, lhs, rhs, out, scale

    def each(self, t, body):
        kind = jnp.where(t < 6, t % 2, 2)
        for n, axes in enumerate(ORDERS):
            pl.when(kind == n)(functools.partial(body, axes))

    def view(self, t, sel, rows=ALL):
        return self.own.at[t, sel.get("x", ALL), sel.get("z", ALL), sel.get("y", ALL), rows]

    def copy(self, t, n, src, dst, **move):
        return pltpu.make_async_remote_copy(
            src_ref=src, dst_ref=dst, send_sem=self.send.at[t, n], recv_sem=self.recv.at[t, n],
            device_id=device(self.spot, **move), device_id_type=MESH)

    def pair(self, t):
        return self.copy(t, 0, self.pair_out.at[t % 3], self.own.at[t], c=1)

    def parts(self, t, phase, axes):
        axis = axes[phase]
        me = self.spot[axis]
        fixed = {a: self.spot[a] for a in axes[:phase]}
        chunk = lambda by: {**fixed, axis: (me + by) % 4}
        second = (self.r2, self.s2, self.t2)[phase]
        n = 1 + 4 * phase
        mine = self.view(t, chunk(0))
        if phase:
            def copies(i):
                return self.copy(t, n + i, self.view(t, chunk(i + 1)), second.at[t, i], **{axis: i + 1})

            return copies, (None, None, mine), (None, second.at[t])
        rest = [a for a in "xzy" if a != axis][0]
        half = lambda by, k: self.view(t, {**chunk(by), rest: pl.ds(2 * k, 2)})

        def copies(i):
            src = (half(2, 0), half(2, 1), self.view(t, chunk(1)), self.view(t, chunk(3)))[i]
            dst = (self.r1, self.r1, second, second)[i].at[t, i % 2]
            return self.copy(t, n + i, src, dst, **{axis: 1 + 2 * (i % 2)})

        return copies, (half(1, 0), half(3, 1), mine), (self.r1.at[t], second.at[t])

    def partner_tile(self, t):
        pl.when(t >= 3)(lambda: self.pair(t - 3).wait_send())
        c = self.spot["c"]
        for xx in range(4):
            got = dot(self.lhs[xx, 1 - c], self.rhs[:, lanes(t, WIDE)])
            self.pair_out[t % 3, xx] = got.reshape(4, 4, 16, WIDE)
        self.pair(t).start()

    def own_tile(self, t):
        c = self.spot["c"]
        self.pair(t).wait_recv()
        for xx in range(4):
            got = dot(self.lhs[xx, c], self.rhs[:, lanes(t, WIDE)])
            self.own[t, xx] = self.own[t, xx] + got.reshape(4, 4, 16, WIDE)
        self.each(t, functools.partial(self.begin, t, 0))

    def begin(self, t, phase, axes):
        copies, _, _ = self.parts(t, phase, axes)
        for i in (1, 0, 2) if phase else (0, 1):
            copies(i).start()

    def pass_on(self, t):
        def body(axes):
            copies, (after, before, _), (first, _) = self.parts(t, 0, axes)
            copies(0).wait_recv()
            after[...] = after[...] + first[0]
            copies(2).start()
            copies(1).wait_recv()
            before[...] = before[...] + first[1]
            copies(3).start()

        self.each(t, body)

    def finish(self, t, phase):
        def body(axes):
            copies, (_, _, mine), (_, second) = self.parts(t, phase, axes)
            for i in range(3) if phase else (2, 3):
                copies(i).wait_recv()
            total = mine[...] + second[0] + second[1]
            if phase:
                total = total + second[2]
            if phase == 2:
                self.out[:, lanes(t, WIDE)] = total * self.scale
            else:
                mine[...] = total
                self.begin(t, phase + 1, axes)

        self.each(t, body)

    def drain(self):
        @pl.loop(0, TILES)
        def _(t):
            pl.when(t >= TILES - 3)(lambda: self.pair(t).wait_send())

            def body(axes):
                for phase in range(3):
                    for i in range(3 if phase else 4):
                        self.parts(t, phase, axes)[0](i).wait_send()

            self.each(t, body)

    @staticmethod
    def scratch():
        V = pltpu.VMEM
        return [
            V((TILES, 4, 4, 4, 16, WIDE), f32),
            V((3, 4, 4, 4, 16, WIDE), f32),
            V((TILES, 2, 2, 4, 16, WIDE), f32),
            V((TILES, 2, 4, 4, 16, WIDE), f32),
            V((TILES, 3, 4, 16, WIDE), f32),
            V((TILES, 3, 16, WIDE), f32),
            pltpu.SemaphoreType.DMA((TILES, 13)),
            pltpu.SemaphoreType.DMA((TILES, 13)),
        ]


FLOW = len(Flow.scratch())
SCATTER = len(Scatter.scratch())


def layer(scale, q_in, k_in, v_in, w_in, og_in, res_out, gq_out, gk_out, gv_out, gw_out, *refs):
    (q, k, v, og, g, att, gq, att_t, intra, wrow, wcol, col, tri, tri_t, ctri, ctri_t, crow,
     in_sem, row_sem, col_sem, out_sem) = refs[:21]
    pre_refs, suf_refs, sc_refs = refs[21:21 + FLOW], refs[21 + FLOW:21 + 2 * FLOW], refs[21 + 2 * FLOW:]
    spot = place()
    met = greet(spot)
    c = spot["c"]
    pre, suf = Flow(spot, pre_refs, False), Flow(spot, suf_refs, True)
    scatter = Scatter(spot, att_t, og, gw_out, sc_refs, scale)

    def load(n, src, dst, part):
        cols = pl.ds(pl.multiple_of(part * 1024, 1024), 1024)
        return pltpu.make_async_copy(src.at[:, cols], dst.at[:, cols], in_sem.at[n])

    theirs, ours = 1 - c, c
    loads = {}
    for n, (name, src, dst, part) in enumerate((
            ("k0", k_in, k, theirs), ("v0", v_in, v, theirs), ("k1", k_in, k, ours), ("v1", v_in, v, ours),
            ("q0", q_in, q, theirs), ("q1", q_in, q, ours), ("og0", og_in, og, theirs), ("og1", og_in, og, ours))):
        loads[name] = load(n, src, dst, part)

    def tile_of(p):
        return (p + 4 * theirs) % 8

    def row_tile(p):
        rows = pl.ds(pl.multiple_of(tile_of(p) * WIDE, WIDE), WIDE)
        return pltpu.make_async_copy(w_in.at[rows], wrow.at[p % 3], row_sem.at[p])

    def col_tile(n):
        return pltpu.make_async_copy(w_in.at[:, lanes(n, WIDE)], wcol.at[n % 2], col_sem.at[n])

    for name in ("k0", "v0", "k1", "v1", "q0", "q1"):
        loads[name].start()
    row_tile(0).start()
    loads["og0"].start()
    loads["og1"].start()
    row_tile(1).start()
    row_tile(2).start()

    base = lax.axis_index("seq") * TOK + 1

    def scale_of(shape, dim):
        index = lax.broadcasted_iota(jnp.int32, shape, dim)
        return lax.rsqrt((DH * (index + base)).astype(f32))

    col[...] = scale_of((TOK, DH), 0)
    crow[...] = scale_of((8, TOK), 1)
    below = (lax.broadcasted_iota(jnp.int32, (MID, MID), 0) >= lax.broadcasted_iota(jnp.int32, (MID, MID), 1)).astype(f32)
    above = (lax.broadcasted_iota(jnp.int32, (MID, MID), 0) <= lax.broadcasted_iota(jnp.int32, (MID, MID), 1)).astype(f32)
    tri[...] = below
    for b, rows in enumerate((A, B)):
        ctri[b] = jnp.concatenate([col[rows]] * 2, axis=1) * below
        ctri_t[b] = crow[0:1, rows] * above
    pre.clear()
    suf.clear()
    met()

    def local_state(h):
        pre.local[h] = dot(k[:, lanes(h)].T, v[:, lanes(h)])

    def local_grad(h):
        high, low = two(col[...] * q[:, lanes(h)].astype(f32))
        both = dot(g[:, lanes(h)].T, jnp.concatenate([high, low], axis=1))
        suf.local[h] = both[:, :DH] + both[:, DH:]

    def attend_intra(h):
        hs = lanes(h)
        c_b = jnp.concatenate([col[B]] * 2, axis=1)
        w_a = (dot_nt(q[A, hs], k[A, hs]) * ctri[0]).astype(bf16)
        w_ba = (dot_nt(q[B, hs], k[A, hs]) * c_b).astype(bf16)
        w_bb = (dot_nt(q[B, hs], k[B, hs]) * ctri[1]).astype(bf16)
        intra[h, A] = dot(w_a, v[A, hs])
        intra[h, B] = dot(jnp.concatenate([w_ba, w_bb], axis=1), v[:, hs])

    def attend(h):
        hs = lanes(h)
        high, low = two(pre.state[h])
        x = q[:, hs]
        inter = dot(jnp.concatenate([x, x], axis=1), jnp.concatenate([high, low], axis=0))
        got = (col[...] * inter + intra[h]).astype(bf16)
        att[:, hs] = got
        att_t[h // 4, h % 4 // 2, lanes(h % 2)] = got.T

    def grad_att(p):
        row_tile(p).wait()
        n = tile_of(p)
        g[:, lanes(n, WIDE)] = dot_nt(og[...], wrow[p % 3]).astype(bf16)
        pl.when(p + 3 < TILES)(lambda: row_tile(p + 3).start())

        @pl.loop(0, 2)
        def _(e):
            local_grad(2 * n + e)
            pl.when(p < 4)(lambda: suf.pair(2 * p + e).start())

    def back_q(h):
        hs = lanes(h)
        ga, gb, va, vb = (r[s, hs] for r in (g, v) for s in (A, B))
        gg = g[:, hs]
        r_a = (dot_nt(ga, va) * tri[...]).astype(bf16)
        r_ba = dot_nt(gb, va).astype(bf16)
        r_bb = (dot_nt(gb, vb) * tri[...]).astype(bf16)
        high, low = two(pre.state[h])
        inter = dot_nt(jnp.concatenate([gg, gg], axis=1), jnp.concatenate([high, low], axis=1))
        gq[A, hs] = (col[A] * (inter[:MID] + dot(r_a, k[A, hs]))).astype(bf16)
        gq[B, hs] = (col[B] * (inter[MID:] + dot(jnp.concatenate([r_ba, r_bb], axis=1), k[:, hs]))).astype(bf16)
        head_out(0, h).start()

    def back_kv(h):
        hs = lanes(h)
        ga, gb, va, vb, ka, kb, qa, qb = (r[s, hs] for r in (g, v, k, q) for s in (A, B))
        gg, vv, kk, qq = g[:, hs], v[:, hs], k[:, hs], q[:, hs]
        c_b = crow[0:1, B]
        high, low = two(suf.state[h])
        s_aa = (dot_nt(va, ga) * ctri_t[0]).astype(bf16)
        s_ab = (dot_nt(va, gb) * c_b).astype(bf16)
        s_bb = (dot_nt(vb, gb) * ctri_t[1]).astype(bf16)
        inter = dot(jnp.concatenate([vv, vv], axis=1), jnp.concatenate([high, low], axis=0))
        gk_a = (inter[:MID] + dot(jnp.concatenate([s_aa, s_ab], axis=1), qq)).astype(bf16)
        gk_b = (inter[MID:] + dot(s_bb, qb)).astype(bf16)
        w_aa = (dot_nt(ka, qa) * ctri_t[0]).astype(bf16)
        w_ab = (dot_nt(ka, qb) * c_b).astype(bf16)
        w_bb = (dot_nt(kb, qb) * ctri_t[1]).astype(bf16)
        inter = dot_nt(jnp.concatenate([kk, kk], axis=1), jnp.concatenate([high, low], axis=1))
        gv_a = (inter[:MID] + dot(jnp.concatenate([w_aa, w_ab], axis=1), gg)).astype(bf16)
        gv_b = (inter[MID:] + dot(w_bb, gb)).astype(bf16)
        k[A, hs], k[B, hs] = gk_a, gk_b
        v[A, hs], v[B, hs] = gv_a, gv_b
        for n in (1, 2):
            head_out(n, h).start()

    def head_out(n, h):
        src, dst = ((gq, gq_out), (k, gk_out), (v, gv_out))[n]
        return pltpu.make_async_copy(src.at[:, lanes(h)], dst.at[:, lanes(h)], out_sem.at[n, h])

    def result_out(n):
        return pltpu.make_async_copy(og.at[:, lanes(n, WIDE)], res_out.at[:, lanes(n, WIDE)], out_sem.at[3, n])

    def result(n):
        col_tile(n).wait()
        og[:, lanes(n, WIDE)] = dot(att[...], wcol[n % 2]).astype(bf16)
        result_out(n).start()
        pl.when(n + 2 < TILES)(lambda: col_tile(n + 2).start())

    loads["k0"].wait()
    loads["v0"].wait()
    @pl.loop(0, HALF)
    def _(i):
        local_state(HALF * theirs + i)
        pre.pair(i).start()

    loads["k1"].wait()
    loads["v1"].wait()

    @pl.loop(0, HALF)
    def _(i):
        local_state(HALF * ours + i)
        pl.when(pre.rank == 0)(lambda: pre.step(i))

    for name in ("q0", "q1"):
        loads[name].wait()

    def attend_pair(i, _):
        attend(HALF * c + i)
        pre.share(i).wait_recv()
        attend(HALF * (1 - c) + i)

    def attended(p):
        return jnp.minimum(pre.due(p - 2, -3), jnp.minimum(p // 2, HALF))

    col_tile(0).start()
    col_tile(1).start()
    def attend_due(p):
        lax.fori_loop(attended(p), attended(p + 1), attend_pair, None)

    loads["og0"].wait()
    loads["og1"].wait()

    @pl.loop(0, TILES)
    def _(n):
        pre.steps(2 * n, -1)

        @pl.loop(0, 2)
        def _(e):
            attend_intra(HALF * e + n)

        attend_due(2 * n)
        pre.steps(2 * n + 1, -1)
        grad_att(n)
        attend_due(2 * n + 1)

    suf.steps(0)

    @pl.loop(2 * TILES, 2 * TILES + HALF)
    def _(p):
        pre.steps(p, -1)
        attend_due(p)
        pl.when(p % 2 == 1)(lambda: suf.steps((p - 15) // 2))

    @pl.loop(0, TILES + 6)
    def _(n):
        pl.when(n < TILES)(lambda: scatter.partner_tile(n))
        pl.when(jnp.logical_and(n >= 2, n < TILES + 2))(lambda: scatter.own_tile(n - 2))
        pl.when(n >= 6)(lambda: scatter.pass_on(n - 6))
        first = 5 + 16 * n // 10
        suf.steps(first, slots=5 + 16 * (n + 1) // 10 - first)

        @pl.when(n >= TILES + 2)
        def _():
            pl.loop(0, 2)(lambda e: result(2 * (n - TILES - 2) + e))


    @pl.loop(0, TILES)
    def _(n):
        scatter.finish(n, 0)

        @pl.loop(0, 2)
        def _(e):
            pl.when(e == 1)(lambda: suf.share(n).wait_recv())
            back_q(HALF * ((c + e) % 2) + n)
            back_kv(HALF * ((c + e) % 2) + n)

    for phase in (1, 2):
        pl.loop(0, TILES)(lambda n: scatter.finish(n, phase))
    scatter.drain()
    pre.drain()
    suf.drain()
    @pl.loop(0, HEADS)
    def _(h):
        for n in range(3):
            head_out(n, h).wait()

    pl.loop(0, TILES)(lambda n: result_out(n).wait())


def local(queries, keys, values, out_weight, out_grad):
    tokens = lax.axis_size("dp") * lax.axis_size("seq") * TOK
    wide = lambda: pltpu.VMEM((TOK, HD), bf16)
    hbm = pl.BlockSpec(memory_space=pl.ANY)
    rows = jax.ShapeDtypeStruct((TOK, HD), bf16)
    sem = pltpu.SemaphoreType.DMA
    outs = pl.pallas_call(
        functools.partial(layer, float(tokens) ** -0.5),
        out_shape=[rows] * 4 + [jax.ShapeDtypeStruct((16, HD), f32)],
        in_specs=[hbm] * 5,
        out_specs=[hbm] * 4 + [pl.BlockSpec(memory_space=pltpu.VMEM)],
        scratch_shapes=[
            wide(), wide(), wide(), wide(), wide(), wide(), wide(),
            pltpu.VMEM((4, 2, 256, TOK), bf16),
            pltpu.VMEM((HEADS, TOK, DH), f32),
            pltpu.VMEM((3, WIDE, HD), bf16),
            pltpu.VMEM((2, HD, WIDE), bf16),
            pltpu.VMEM((TOK, DH), f32),
            pltpu.VMEM((MID, MID), f32),
            pltpu.VMEM((MID, MID), f32),
            pltpu.VMEM((2, MID, MID), f32),
            pltpu.VMEM((2, MID, MID), f32),
            pltpu.VMEM((8, TOK), f32),
            sem((8,)), sem((TILES,)), sem((TILES,)), sem((4, HEADS)),
        ] + Flow.scratch() + Flow.scratch() + Scatter.scratch(),
        compiler_params=pltpu.CompilerParams(collective_id=0, has_side_effects=True, vmem_limit_bytes=60 * 2**20),
        cost_estimate=pl.CostEstimate(flops=23 * 10**9, bytes_accessed=25 * 10**6, transcendentals=0),
    )(*(x.reshape(TOK, HD) for x in (queries, keys, values)), out_weight, out_grad.reshape(TOK, HD))
    return tuple(x if x.shape[0] == 16 else x.reshape(1, TOK, HD) for x in put(outs))


def put_kernel(*refs):
    ins, outs, held, sem = refs[:5], refs[5:10], refs[10:15], refs[15]
    parts = []
    for n in range(5):
        step = ins[n].shape[0] // 2
        for part in range(2):
            rows = pl.ds(part * step, step)
            parts.append((
                pltpu.make_async_copy(ins[n].at[rows], held[n].at[rows], sem.at[0, n, part]),
                pltpu.make_async_copy(held[n].at[rows], outs[n].at[rows], sem.at[1, n, part])))
    for get, _ in parts:
        get.start()
    for get, give in parts:
        get.wait()
        give.start()
    for _, give in parts:
        give.wait()


def put(arrays):
    hbm = pl.BlockSpec(memory_space=pl.ANY)
    return pl.pallas_call(
        put_kernel,
        out_shape=[jax.ShapeDtypeStruct(x.shape, x.dtype) for x in arrays],
        in_specs=[hbm] * 5,
        out_specs=[hbm] * 5,
        scratch_shapes=[pltpu.VMEM(x.shape, x.dtype) for x in arrays] + [pltpu.SemaphoreType.DMA((2, 5, 2))],
        compiler_params=pltpu.CompilerParams(vmem_limit_bytes=60 * 2**20),
    )(*arrays)


def solution(mesh):
    in_specs = (
        P("dp", "seq", None),
        P("dp", "seq", None),
        P("dp", "seq", None),
        P(),
        P("dp", "seq", None),
    )
    out_specs = (
        P("dp", "seq", None),
        P("dp", "seq", None),
        P("dp", "seq", None),
        P("dp", "seq", None),
        P(("seq", "dp"), None),
    )
    return jax.shard_map(local, mesh=mesh, in_specs=in_specs, out_specs=out_specs, check_vma=False)
```
